32 devices in a mesh: epoch: 4 (over z), prow: 2 (over x), pcol: 4 (over y, core).
Axes of the slice: x: 2, y: 2, z: 4, core: 2. Of those that a mesh axis runs over, the one named last changes fastest.
Arguments:
- steps: int32 [2, 8192], P(None, 'epoch'), may hold values from 0 to 47
- harmonic: int32 [4096], replicated, may hold values from 0 to 4095, each once
- col_scale: float32 [4096], replicated, may hold values from 0.3 to 3
- taps: float32 [256], replicated, may hold values from -0.375 to 0.375
- ridge: float32 [4096], P(('epoch', 'prow')), may hold values from 0.1 to 1
Outputs:
- panel: float32 [4096, 256], P(('epoch', 'prow'))
- schur: float32 [4096, 4096], P(('epoch', 'prow'), 'pcol')
The draws below stay inside these ranges and needn't reach their ends.
Inputs may be any that keep to these rules, and one draw needn't show every extreme that they name: `harmonic`: each of 0 to 4095 once.
All inputs are finite; a program needn't handle non-finite values.
Results may differ from the reference program's by a relative error of at most 0.0028.
Values may be sent and summed in bfloat16 or wider, within the bound.
No kernel may reach another device: no remote copies, remote signals or barrier semaphores. Data moves between devices by JAX's collectives and lax.ppermute only.
A program may use at most 128 MiB of HBM per device.

```python
import math
import jax
import jax.numpy as jnp
from jax import lax

P_SIZE = 4096
B = 256
TAPS = 256
EPOCHS = 8192


def place_ends(drawn, own_key, least, top_value):
    dims = drawn.shape
    place = [jax.random.randint(jax.random.fold_in(own_key, axis), (), 0, dims[axis]) for axis in range(len(dims))]
    drawn = drawn.at[tuple(place)].set(least)
    longest = dims.index(max(dims))
    place[longest] = (place[longest] + 1) % dims[longest]
    return drawn.at[tuple(place)].set(top_value)


def block_levels(own_key, extent, shards, smallest, largest):
    level = 1.0
    for dim, blocks in shards:
        draws = jax.random.uniform(jax.random.fold_in(jax.random.fold_in(own_key, 6), dim), (blocks,), jnp.float32, smallest / len(shards), largest / len(shards))
        level = level * jnp.repeat(jnp.exp(draws), extent[dim] // blocks).reshape((-1,) + (1,) * (len(extent) - 1 - dim))
    return level


def normal_values(own_key, shape, spread, reach, kind=jnp.bfloat16):
    return jnp.clip(spread * jax.random.normal(own_key, shape, jnp.float32), -reach, reach).astype(kind)


def setup_inputs(seed: int = 0) -> dict:
    seeds = jax.random.split(jax.random.key(seed), 6)
    return {
        "steps": place_ends(jax.random.randint(seeds[0], (2, EPOCHS), 0, 48), jax.random.fold_in(seeds[0], 1), 0, 47).astype(jnp.int32),
        "harmonic": jax.random.permutation(seeds[1], P_SIZE).astype(jnp.int32),
        "col_scale": jnp.clip(jnp.exp(jax.random.uniform(seeds[2], (P_SIZE,), jnp.float32, math.log(0.3), math.log(3.0))), 0.3, 3.0),
        "taps": normal_values(seeds[3], (TAPS,), TAPS ** -0.5, 0.375, jnp.float32),
        "ridge": jnp.clip(jnp.exp(math.log(1.0) - 2.3025851 * jax.random.uniform(seeds[4], (P_SIZE,), jnp.float32) ** block_levels(seeds[4], (P_SIZE,), ((0, 8),), -0.2, 0.2)), 0.1, 1.0),
    }


phase_count = 4096
angle_step = 2.0 * math.pi / 4096.0

def toeplitz_pair(taps):
    count = taps.shape[0]
    pattern = jnp.concatenate([jnp.zeros((1,), jnp.float32), taps[::-1], jnp.zeros((count,), jnp.float32)])
    full = jnp.tile(pattern, count)[:2 * count * count].reshape(count, 2 * count).astype(jnp.bfloat16)
    return (full[:, :count], full[:, count:])

def harmonic_design(phase_first, phase_second, orders, degrees, scales):
    indices = (phase_first[:, None] * orders[None, :] + phase_second[:, None] * degrees[None, :]) % phase_count
    angle = indices.astype(jnp.float32) * angle_step
    return (jnp.cos(angle) + jnp.sin(angle)) * scales[None, :]

def reference(steps, harmonic, col_scale, taps, ridge):
    phase = (jnp.cumsum(steps, axis=1) % phase_count).astype(jnp.int32)
    orders = (harmonic // 64).astype(jnp.int32)
    degrees = (harmonic % 64).astype(jnp.int32)
    design = harmonic_design(phase[0], phase[1], orders, degrees, col_scale).astype(jnp.bfloat16)
    joined = jnp.concatenate([jnp.zeros((TAPS, P_SIZE), jnp.bfloat16), design], axis=0)
    blocks = EPOCHS // TAPS
    earlier_rows = joined[:EPOCHS].reshape(blocks, TAPS, P_SIZE).astype(jnp.float32)
    current_rows = joined[TAPS:].reshape(blocks, TAPS, P_SIZE).astype(jnp.float32)
    lower_part, upper_part = toeplitz_pair(taps)
    filtered = jnp.einsum('ij,bjc->bic', lower_part.astype(jnp.float32), earlier_rows)
    filtered = filtered + jnp.einsum('ij,bjc->bic', upper_part.astype(jnp.float32), current_rows)
    filtered = filtered.reshape(EPOCHS, P_SIZE).astype(jnp.bfloat16)
    normal = jnp.dot(filtered.T.astype(jnp.float32), filtered.astype(jnp.float32), preferred_element_type=jnp.float32) / EPOCHS
    normal = normal + jnp.diag(ridge)
    leading = jnp.linalg.cholesky(normal[:B, :B])
    panel = jax.scipy.linalg.solve_triangular(leading, normal[:, :B].T, lower=True).T
    schur = normal - jnp.dot(panel.astype(jnp.float32), panel.T.astype(jnp.float32), precision=lax.Precision.HIGHEST, preferred_element_type=jnp.float32)
    return (panel, schur)
```

```python
import functools
import math

import jax
import jax.numpy as jnp
from jax import lax
from jax.experimental import pallas as pl
from jax.experimental.pallas import tpu as pltpu
from jax.sharding import PartitionSpec as P

B = 256

phase_count = 4096
SINE = (6.2831640442776635, -41.337142367123384, 81.34076873476997, -70.99343163979194)


def rotated(x, axis):
    count = lax.axis_size(axis)
    shifts = [[(i, (i + k) % count) for i in range(count)] for k in range(1, count)]
    return [x] + [lax.ppermute(x, axis, pairs) for pairs in shifts]


def gathered_doubling(x, axes):
    count, mine = lax.axis_size(axes), lax.axis_index(axes)
    size, held, have = x.shape[0], x, 1
    while have < count:
        take = min(have, count - have)
        pairs = [((i + have) % count, i) for i in range(count)]
        held = jnp.concatenate([held, lax.ppermute(held[: take * size], axes, pairs)])
        have += take
    return jnp.roll(held, mine * size)


def toeplitz_transposed(taps):
    count = taps.shape[0]
    pattern = jnp.concatenate(
        [jnp.zeros((1,), jnp.float32), taps[::-1], jnp.zeros((count,), jnp.float32)]
    )
    full = (
        jnp.tile(pattern, count)[: 2 * count * count].reshape(count, 2 * count).astype(jnp.bfloat16)
    )
    return full.T


def pick_chunk(width):
    for size in (256, 224, 192, 160, 128, 96, 64, 48, 32, 16):
        if width % size == 0:
            return size
    return width


def split3(x):
    high = x.astype(jnp.bfloat16)
    rest = x - high.astype(jnp.float32)
    mid = rest.astype(jnp.bfloat16)
    return high, mid, (rest - mid.astype(jnp.float32)).astype(jnp.bfloat16)


def dot_f32(a, b, b_dim):
    ah, am, al = split3(a)
    bh, bm, bl = split3(b)
    return lax.dot_general(
        jnp.concatenate([ah, ah, am, ah, al, am], axis=1),
        jnp.concatenate([bh, bm, bh, bl, bh, bm], axis=b_dim),
        (((1,), (b_dim,)), ((), ())),
        preferred_element_type=jnp.float32,
    )


def factor_panel(t, size, group):
    row = lax.broadcasted_iota(jnp.int32, t.shape, 0)
    for j in range(0, size, group):
        span = range(group)
        cols = [jnp.broadcast_to(t[:, j + k : j + k + 1], t.shape) for k in span]
        rows = [t[j + k : j + k + 1, :] for k in span]
        pivot = [[cols[l][j + k : j + k + 1, :] for l in span] for k in span]
        done = []
        for k in span:
            root = lax.rsqrt(pivot[k][k])
            inverse = root * root
            weight = rows[k] * inverse
            for l in range(k + 1, group):
                lower = pivot[l][k]
                rows[l] = rows[l] - lower * weight
                cols[l] = cols[l] - cols[k] * (pivot[k][l] * inverse)
                for q in range(k + 1, group):
                    pivot[l][q] = pivot[l][q] - lower * (pivot[k][q] * inverse)
            t = t - jnp.where(row >= j + group, cols[k], 0.0) * weight
            done.append(rows[k] * root)
        for k in span:
            t = jnp.where(row == j + k, done[k], t)
    return t


def invert_factor(m_ref, size, group):
    n = m_ref.shape[0]

    @pl.loop(0, n // size)
    def _(k):
        here = pl.ds(pl.multiple_of(k * size, size), size)
        panel = m_ref[here, :]
        lane = lax.broadcasted_iota(jnp.int32, (size, 2 * size), 1)
        row = lax.broadcasted_iota(jnp.int32, (size, 2 * size), 0)
        eye = jnp.where(lane == row, 1.0, 0.0)
        t = jnp.where(
            lane < size, panel[:, : 2 * size], jnp.where(lane - size == row, 1.0, 0.0)
        )
        t = factor_panel(t, size, group)
        inverse = pltpu.roll(t, size, 1)[:, :size]
        first = jnp.where(lane < size, eye, panel[:, : 2 * size])
        done = dot_f32(inverse, jnp.concatenate([first, panel[:, 2 * size :]], axis=1), 0)
        full = m_ref[...]
        below = lax.broadcasted_iota(jnp.int32, (n, size), 0) >= (k + 1) * size
        low = jnp.where(below, dot_f32(full[:, :size], inverse, 1), 0.0)
        kept = jnp.where(lax.broadcasted_iota(jnp.int32, (n, n), 1) < size, 0.0, full)
        m_ref[...] = pltpu.roll(kept - dot_f32(low, done, 0), n - size, 1)
        m_ref[here, :] = pltpu.roll(done, n - size, 1)


def fill_phases(mine, steps_refs, sums_ref, pt_ref):
    here = steps_refs[0].shape[1]
    blocks = here // 128
    count = len(steps_refs)
    for k, ref in enumerate(steps_refs):
        group = lax.rem(mine - k + count, count)
        for b in range(blocks):
            row = pl.multiple_of((group * blocks + b) * 2, 2)
            sums_ref[pl.ds(row, 2), :] = ref[:, b * 128 : (b + 1) * 128].astype(jnp.float32)
    total = sums_ref.shape[0]
    terms = sums_ref[...].astype(jnp.bfloat16)
    i = lax.broadcasted_iota(jnp.int32, (128, 128), 0)
    j = lax.broadcasted_iota(jnp.int32, (128, 128), 1)
    inside = jnp.dot(
        terms, jnp.where(i <= j, 1.0, 0.0).astype(jnp.bfloat16), preferred_element_type=jnp.float32
    )
    ends = jnp.dot(terms, jnp.ones((128, 128), jnp.bfloat16), preferred_element_type=jnp.float32)
    ends = ends.astype(jnp.int32)
    i = lax.broadcasted_iota(jnp.int32, (total, total), 0)
    j = lax.broadcasted_iota(jnp.int32, (total, total), 1)
    earlier = jnp.where((j < i) & ((i - j) % 2 == 0), 1.0, 0.0).astype(jnp.bfloat16)

    def before(x):
        return jnp.dot(
            earlier, x.astype(jnp.float32).astype(jnp.bfloat16), preferred_element_type=jnp.float32
        ).astype(jnp.int32)

    phase = inside.astype(jnp.int32) + before(ends & 127) + before(ends >> 7) * 128
    phase = phase & (phase_count - 1)
    high = (phase & 4032).astype(jnp.float32) * (1.0 / phase_count)
    low = (phase & 63).astype(jnp.float32) * (1.0 / phase_count)
    pt_ref[...] = jnp.zeros_like(pt_ref)
    pt_ref[4:5, :] = jnp.full((1, pt_ref.shape[1]), -0.125, jnp.float32)
    for b in range(total // 2):
        pt_ref[0:2, b * 128 : (b + 1) * 128] = high[2 * b : 2 * b + 2, :]
        pt_ref[2:4, b * 128 : (b + 1) * 128] = low[2 * b : 2 * b + 2, :]


def normal_kernel(shape, chunk, n_steps, *refs):
    rows, lead, cols, n_row = shape
    steps_refs = refs[:n_steps]
    params_ref, wt_ref, panel_ref, schur_ref = refs[n_steps : n_steps + 4]
    d_ref, f_ref, acc_ref, sums_ref, pt_ref, h_ref, m_ref = refs[n_steps + 4 :]
    width, tile = f_ref.shape
    count = wt_ref.shape[1]
    step = pl.program_id(0)
    total = pl.num_programs(0) * tile

    @pl.when(step == 0)
    def _():
        fill_phases(lax.axis_index("epoch"), steps_refs, sums_ref, pt_ref)
        h_ref[...] = jnp.concatenate(
            [params_ref[...], jnp.zeros((120, params_ref.shape[1]), jnp.float32)]
        ).T
        d_ref[:, :count] = jnp.zeros((width, count), jnp.bfloat16)
        acc_ref[...] = jnp.zeros_like(acc_ref)

    @pl.when(step > 0)
    def _():
        d_ref[:, :count] = d_ref[:, tile:]

    pt = pt_ref[:, pl.ds(pl.multiple_of(step * tile, tile), tile)].astype(jnp.bfloat16)

    @pl.loop(0, width // chunk)
    def _(part):
        here = pl.ds(pl.multiple_of(part * chunk, chunk), chunk)
        h = h_ref[here, :]
        turns = jnp.dot(h[:, :16].astype(jnp.bfloat16), pt, preferred_element_type=jnp.float32)
        turns = turns - jnp.round(turns)
        s = 0.25 - jnp.abs(turns)
        z = s * s
        poly = SINE[0] + z * (SINE[1] + z * (SINE[2] + z * SINE[3]))
        d_ref[here, count:] = ((s * poly) * h[:, 5:6]).astype(jnp.bfloat16)
        for b in range(tile // count):
            f_ref[here, b * count : (b + 1) * count] = jnp.dot(
                d_ref[here, b * count : (b + 2) * count],
                wt_ref[...],
                preferred_element_type=jnp.float32,
            ).astype(jnp.bfloat16)

    acc_ref[...] += lax.dot_general(
        f_ref[: rows + lead, :],
        f_ref[rows:, :],
        (((1,), (1,)), ((), ())),
        preferred_element_type=jnp.float32,
    )

    @pl.when(step == pl.num_programs(0) - 1)
    def _():
        first_row = (lax.axis_index("epoch") * n_row + lax.axis_index("prow")) * rows
        first_col = lax.axis_index("pcol") * cols
        i = lax.broadcasted_iota(jnp.int32, acc_ref.shape, 0)
        j = lax.broadcasted_iota(jnp.int32, acc_ref.shape, 1)
        i = jnp.where(i < rows, i + first_row, i - rows)
        j = jnp.where(j < lead, j, j - lead + first_col)
        acc_ref[...] = acc_ref[...] * (1.0 / total) + jnp.where(
            i == j, h_ref[: rows + lead, 6:7], 0.0
        )
        m_ref[...] = acc_ref[rows:, :lead]
        invert_factor(m_ref, 64, 8)
        i = lax.broadcasted_iota(jnp.int32, (lead, lead), 0)
        j = lax.broadcasted_iota(jnp.int32, (lead, lead), 1)
        inverse = jnp.where(i >= j, m_ref[...], 0.0)
        highest = functools.partial(
            lax.dot_general, precision=lax.Precision.HIGHEST, preferred_element_type=jnp.float32
        )
        panel_ref[...] = highest(acc_ref[:rows, :lead], inverse, (((1,), (1,)), ((), ())))
        for c in range(0, cols, 256):
            solved = highest(inverse, acc_ref[rows:, lead + c : lead + c + 256], (((1,), (0,)), ((), ())))
            schur_ref[:, c : c + 256] = acc_ref[:rows, lead + c : lead + c + 256] - highest(
                panel_ref[...], solved, (((1,), (0,)), ((), ()))
            )


def on_device(steps, harmonic, col_scale, taps, ridge):
    params = harmonic.shape[0]
    n_epoch = lax.axis_size("epoch")
    n_row = lax.axis_size("prow")
    n_col = lax.axis_size("pcol")
    rows = params // (n_epoch * n_row)
    cols = params // n_col
    first_row = (lax.axis_index("epoch") * n_row + lax.axis_index("prow")) * rows
    first_col = lax.axis_index("pcol") * cols
    steps_parts = rotated(steps, "epoch")
    ridge_lead = gathered_doubling(ridge, ("epoch", "prow"))[:B]
    width = rows + B + cols
    padded = -(-width // 128) * 128
    epochs = steps.shape[1] * n_epoch
    count = taps.shape[0]
    tile = 1024 if epochs % 1024 == 0 else count

    def own(x):
        return jnp.concatenate(
            [
                lax.dynamic_slice_in_dim(x, first_row, rows),
                x[:B],
                lax.dynamic_slice_in_dim(x, first_col, cols),
                jnp.zeros((padded - width,), x.dtype),
            ]
        )

    harm = own(harmonic)
    orders = (harm // 64).astype(jnp.float32)
    degrees = (harm % 64).astype(jnp.float32)
    ones = jnp.ones_like(orders)
    ridge_rows = jnp.concatenate([ridge, ridge_lead, jnp.zeros((padded - rows - B,), jnp.float32)])
    table = jnp.stack(
        [orders, degrees, orders, degrees, ones, own(col_scale) * math.sqrt(2.0), ridge_rows, 0 * ones]
    )
    whole = lambda i: (0, 0)
    vmem = lambda x: pl.BlockSpec(x.shape, whole)
    operands = (*steps_parts, table, toeplitz_transposed(taps))
    return pl.pallas_call(
        functools.partial(normal_kernel, (rows, B, cols, n_row), pick_chunk(width), len(steps_parts)),
        grid=(epochs // tile,),
        out_shape=(
            jax.ShapeDtypeStruct((rows, B), jnp.float32),
            jax.ShapeDtypeStruct((rows, cols), jnp.float32),
        ),
        in_specs=[vmem(x) for x in operands],
        out_specs=(pl.BlockSpec((rows, B), whole), pl.BlockSpec((rows, cols), whole)),
        scratch_shapes=[
            pltpu.VMEM((width, count + tile), jnp.bfloat16),
            pltpu.VMEM((width, tile), jnp.bfloat16),
            pltpu.VMEM((rows + B, B + cols), jnp.float32),
            pltpu.VMEM((2 * epochs // 128, 128), jnp.float32),
            pltpu.VMEM((16, epochs), jnp.float32),
            pltpu.VMEM((padded, 128), jnp.float32),
            pltpu.VMEM((B, B), jnp.float32),
        ],
        compiler_params=pltpu.CompilerParams(vmem_limit_bytes=56 * 1024 * 1024),
    )(*operands)


def solution(mesh):
    in_specs = (P(None, "epoch"), P(), P(), P(), P(("epoch", "prow")))
    out_specs = (P(("epoch", "prow"), None), P(("epoch", "prow"), "pcol"))
    return jax.shard_map(
        on_device, mesh=mesh, in_specs=in_specs, out_specs=out_specs, check_vma=False
    )
```

```python
import functools
import math

import jax
import jax.numpy as jnp
from jax import lax
from jax.experimental import pallas as pl
from jax.experimental.pallas import tpu as pltpu
from jax.sharding import PartitionSpec as P

B = 256

phase_count = 4096
SINE = (6.2831640442776635, -41.337142367123384, 81.34076873476997, -70.99343163979194)
LEAD = SINE[3]
POLY = tuple(c / LEAD for c in SINE[:3])
VMEM_LIMIT = 58 * 1024 * 1024


def rotated(x, axis):
    count = lax.axis_size(axis)
    shifts = [[(i, (i + k) % count) for i in range(count)] for k in range(1, count)]
    return [x] + [lax.ppermute(x, axis, pairs) for pairs in shifts]


def gathered_doubling(x, axes):
    count = lax.axis_size(axes)
    held, have = x[None], 1
    while have < count:
        take = min(have, count - have)
        pairs = [((i + have) % count, i) for i in range(count)]
        held = jnp.concatenate([held, lax.ppermute(held[:take], axes, pairs)])
        have += take
    return held


def split3(x):
    high = x.astype(jnp.bfloat16)
    rest = x - high.astype(jnp.float32)
    mid = rest.astype(jnp.bfloat16)
    return high, mid, (rest - mid.astype(jnp.float32)).astype(jnp.bfloat16)


def dot_f32(a, b, b_dim):
    ah, am, al = split3(a)
    bh, bm, bl = split3(b)
    return lax.dot_general(
        jnp.concatenate([ah, ah, am, ah, al, am], axis=1),
        jnp.concatenate([bh, bm, bh, bl, bh, bm], axis=b_dim),
        (((1,), (b_dim,)), ((), ())),
        preferred_element_type=jnp.float32,
    )


def factor_panel(t, size, group):
    row = lax.broadcasted_iota(jnp.int32, t.shape, 0)
    for j in range(0, size, group):
        span = range(group)
        cols = [jnp.broadcast_to(t[:, j + k : j + k + 1], t.shape) for k in span]
        rows = [t[j + k : j + k + 1, :] for k in span]
        pivot = [[cols[l][j + k : j + k + 1, :] for l in span] for k in span]
        done = []
        for k in span:
            root = lax.rsqrt(pivot[k][k])
            inverse = root * root
            weight = rows[k] * inverse
            for l in range(k + 1, group):
                lower = pivot[l][k]
                rows[l] = rows[l] - lower * weight
                cols[l] = cols[l] - cols[k] * (pivot[k][l] * inverse)
                for q in range(k + 1, group):
                    pivot[l][q] = pivot[l][q] - lower * (pivot[k][q] * inverse)
            t = t - jnp.where(row >= j + group, cols[k], 0.0) * weight
            done.append(rows[k] * root)
        for k in span:
            t = jnp.where(row == j + k, done[k], t)
    return t


def invert_factor(m_ref, size, group):
    n = m_ref.shape[0]

    @pl.loop(0, n // size)
    def _(k):
        here = pl.ds(pl.multiple_of(k * size, size), size)
        panel = m_ref[here, :]
        lane = lax.broadcasted_iota(jnp.int32, (size, 2 * size), 1)
        row = lax.broadcasted_iota(jnp.int32, (size, 2 * size), 0)
        eye = jnp.where(lane == row, 1.0, 0.0)
        t = jnp.where(
            lane < size, panel[:, : 2 * size], jnp.where(lane - size == row, 1.0, 0.0)
        )
        t = factor_panel(t, size, group)
        inverse = pltpu.roll(t, size, 1)[:, :size]
        first = jnp.where(lane < size, eye, panel[:, : 2 * size])
        done = dot_f32(inverse, jnp.concatenate([first, panel[:, 2 * size :]], axis=1), 0)
        full = m_ref[...]
        below = lax.broadcasted_iota(jnp.int32, (n, size), 0) >= (k + 1) * size
        low = jnp.where(below, dot_f32(full[:, :size], inverse, 1), 0.0)
        kept = jnp.where(lax.broadcasted_iota(jnp.int32, (n, n), 1) < size, 0.0, full)
        m_ref[...] = pltpu.roll(kept - dot_f32(low, done, 0), n - size, 1)
        m_ref[here, :] = pltpu.roll(done, n - size, 1)


def fill_phases(mine, steps_refs, sums_ref, pt_ref):
    here = steps_refs[0].shape[1]
    blocks = here // 128
    count = len(steps_refs)
    for k, ref in enumerate(steps_refs):
        group = lax.rem(mine - k + count, count)
        for b in range(blocks):
            row = pl.multiple_of((group * blocks + b) * 2, 2)
            sums_ref[pl.ds(row, 2), :] = ref[:, b * 128 : (b + 1) * 128].astype(jnp.float32)
    total = sums_ref.shape[0]
    terms = sums_ref[...].astype(jnp.bfloat16)
    i = lax.broadcasted_iota(jnp.int32, (128, 128), 0)
    j = lax.broadcasted_iota(jnp.int32, (128, 128), 1)
    inside = jnp.dot(
        terms, jnp.where(i <= j, 1.0, 0.0).astype(jnp.bfloat16), preferred_element_type=jnp.float32
    )
    ends = jnp.dot(terms, jnp.ones((128, 128), jnp.bfloat16), preferred_element_type=jnp.float32)
    ends = ends.astype(jnp.int32)
    i = lax.broadcasted_iota(jnp.int32, (total, total), 0)
    j = lax.broadcasted_iota(jnp.int32, (total, total), 1)
    earlier = jnp.where((j < i) & ((i - j) % 2 == 0), 1.0, 0.0).astype(jnp.bfloat16)

    def before(x):
        return jnp.dot(
            earlier, x.astype(jnp.float32).astype(jnp.bfloat16), preferred_element_type=jnp.float32
        ).astype(jnp.int32)

    phase = inside.astype(jnp.int32) + before(ends & 127) + before(ends >> 7) * 128
    turn = (phase & (phase_count - 1)).astype(jnp.float32) * (1.0 / phase_count)
    pt_ref[...] = jnp.zeros_like(pt_ref)
    for b in range(total // 2):
        pt_ref[0:2, b * 128 : (b + 1) * 128] = turn[2 * b : 2 * b + 2, :]


def fill_toeplitz(taps_ref, wt_ref):
    count = taps_ref.shape[1]
    taps = taps_ref[...]
    none = jnp.zeros_like(taps)
    for half, row in enumerate(([none, taps], [taps, none])):
        spread = jnp.broadcast_to(jnp.concatenate(row, axis=1), (count, 2 * count))
        spread = pltpu.roll(spread, 0, 1, stride=1, stride_axis=0)
        wt_ref[half * count : (half + 1) * count, :] = spread[:, :count].astype(jnp.bfloat16)


def parameter_table(harmonic, col_scale):
    rows = [harmonic >> 6, harmonic & 63]
    rows = [x.astype(jnp.float32) for x in rows] + [col_scale * (math.sqrt(2.0) * LEAD)]
    return jnp.concatenate(rows + [jnp.zeros((125, harmonic.shape[1]), jnp.float32)]).T


def fill_design(h_ref, pt_ref, d_ref, start, stop, lane, tile):
    here = slice(start, stop)
    p0 = pt_ref[0:1, pl.ds(tile, 256)]
    p1 = pt_ref[1:2, pl.ds(tile, 256)]
    turns = h_ref[here, 0:1] * p0 + h_ref[here, 1:2] * p1 - 0.125
    s = 0.25 - jnp.abs(turns - jnp.round(turns))
    z = s * s
    poly = ((z + POLY[2]) * z + POLY[1]) * z + POLY[0]
    d_ref[here, lane : lane + 256] = (poly * (s * h_ref[here, 2:3])).astype(jnp.bfloat16)


def fill_filtered(d_ref, wt_ref, f_ref, start, stop, block):
    count = wt_ref.shape[1]
    f_ref[start:stop, block * count : (block + 1) * count] = jnp.dot(
        d_ref[start:stop, block * count : (block + 2) * count],
        wt_ref[...],
        preferred_element_type=jnp.float32,
    ).astype(jnp.bfloat16)


def lead_kernel(n_steps, *refs):
    steps_refs = refs[:n_steps]
    harmonic_ref, scale_ref, taps_ref = refs[n_steps : n_steps + 3]
    pt_ref, wt_ref, lead_ref, block_ref = refs[n_steps + 3 : n_steps + 7]
    sums_ref, h_ref, d_ref, f_ref = refs[n_steps + 7 :]
    lead, epochs = lead_ref.shape
    count = wt_ref.shape[1]
    tile = f_ref.shape[1]
    fill_phases(lax.axis_index("epoch"), steps_refs, sums_ref, pt_ref)
    fill_toeplitz(taps_ref, wt_ref)
    h_ref[...] = parameter_table(harmonic_ref[:, :lead], scale_ref[:, :lead])
    d_ref[:, :count] = jnp.zeros((lead, count), jnp.bfloat16)
    block_ref[...] = jnp.zeros_like(block_ref)

    def design(start, row):
        def step():
            for lane in range(0, tile, 256):
                fill_design(h_ref, pt_ref, d_ref, row, row + 16, count + lane, start + lane)
        return step

    for row in range(0, lead, 16):
        design(0, row)()

    @pl.loop(0, epochs // tile)
    def _(step):
        begin = pl.multiple_of(step * tile, tile)
        for b in range(tile // count):
            fill_filtered(d_ref, wt_ref, f_ref, 0, lead, b)
        lead_ref[:, pl.ds(begin, tile)] = f_ref[...]
        d_ref[:, :count] = d_ref[:, tile:]
        following = pl.multiple_of(lax.rem(begin + tile, epochs), tile)
        for row in range(0, lead, 16):
            design(following, row)()
        block_ref[...] += lax.dot_general(
            f_ref[...], f_ref[...], (((1,), (1,)), ((), ())), preferred_element_type=jnp.float32
        )


def main_kernel(shape, *refs):
    rows, lead, cols, n_row = shape
    harmonic_ref, scale_ref, ridge_ref, held_ref, pt_ref, wt_ref, lead_ref, block_ref = refs[:8]
    panel_ref, schur_ref, h_ref, r_ref, d_ref, fa_ref, fb_ref, acc_ref, m_ref = refs[8:]
    width, tile = fa_ref.shape
    count = wt_ref.shape[1]
    step = pl.program_id(0)
    epochs = pt_ref.shape[1]
    mine = lax.axis_index("epoch") * n_row + lax.axis_index("prow")
    first_row = pl.multiple_of(mine * rows, rows)
    first_col = pl.multiple_of(lax.axis_index("pcol") * cols, cols)
    segments = [(0, rows), (rows + lead, width)]

    def design(start, row):
        def run():
            d_ref[row : row + 16, :count] = d_ref[row : row + 16, tile:]
            for lane in range(0, tile, 256):
                fill_design(h_ref, pt_ref, d_ref, row, row + 16, count + lane, start + lane)
        return run

    def filtered(f_ref, begin, end, block):
        return lambda: fill_filtered(d_ref, wt_ref, f_ref, begin, end, block)

    def product(f_ref, begin, end, depth):
        def run():
            acc_ref[:depth, begin:end] += lax.dot_general(
                f_ref[:depth, :],
                f_ref[rows + begin : rows + end, :],
                (((1,), (1,)), ((), ())),
                preferred_element_type=jnp.float32,
            )
        return run

    def products(f_ref):
        pieces = [(0, lead, rows)]
        pieces += [(c, min(c + 256, lead + cols), rows + lead) for c in range(lead, lead + cols, 256)]
        return [product(f_ref, *piece) for piece in pieces]

    @pl.when(step == 0)
    def _():
        table = parameter_table(harmonic_ref[...], scale_ref[...])
        r_ref[...] = table
        h_ref[:rows, :] = r_ref[pl.ds(first_row, rows), :]
        h_ref[rows + lead :, :] = r_ref[pl.ds(first_col, cols), :]
        fb_ref[...] = jnp.zeros_like(fb_ref)
        acc_ref[...] = jnp.zeros_like(acc_ref)
        d_ref[...] = jnp.zeros_like(d_ref)
        for begin, end in segments:
            for row in range(begin, end, 16):
                design(0, row)()

    def phase(f_ref, before_ref, tile_index):
        begin = pl.multiple_of(tile_index * tile, tile)
        following = pl.multiple_of(lax.rem(begin + tile, epochs), tile)
        f_ref[rows : rows + lead, :] = lead_ref[:, pl.ds(begin, tile)]
        chunk = 256
        sets = []
        for start, stop in segments:
            for at in range(start, stop, chunk):
                sets.append((at, min(at + chunk, stop)))
        later = products(before_ref)
        for k, (at, end) in enumerate(sets):
            for b in range(tile // count):
                filtered(f_ref, at, end, b)()
            for n in range(k * len(later) // len(sets), (k + 1) * len(later) // len(sets)):
                later[n]()
            for row in range(at, end, 16):
                design(following, row)()

    phase(fa_ref, fb_ref, 2 * step)
    phase(fb_ref, fa_ref, 2 * step + 1)

    @pl.when(step == pl.num_programs(0) - 1)
    def _():
        for run in products(fb_ref):
            run()
        blocks = held_ref.shape[0]
        mid = -(-rows // 128) * 128
        spare = jnp.zeros((1, mid - rows), jnp.float32) if mid > rows else None
        own = ridge_ref[...] if spare is None else jnp.concatenate([ridge_ref[...], spare], axis=1)
        own = jnp.concatenate([own, jnp.zeros((127, mid), jnp.float32)]).T[:rows, :1]
        first = []
        for q in range(-(-lead // rows)):
            first.append(held_ref[pl.ds(lax.rem(q - mine + blocks, blocks), 1), :])
        first = jnp.concatenate(first, axis=1)[:, :lead]
        first = jnp.concatenate([first, jnp.zeros((127, lead), jnp.float32)]).T[:, :1]
        scale = 1.0 / epochs
        i = lax.broadcasted_iota(jnp.int32, (rows, lead + cols), 0) + first_row
        j = lax.broadcasted_iota(jnp.int32, (rows, lead + cols), 1)
        j = jnp.where(j < lead, j, j - lead + first_col)
        acc_ref[:rows, :] = acc_ref[:rows, :] * scale + jnp.where(i == j, own, 0.0)
        i = lax.broadcasted_iota(jnp.int32, (lead, cols), 0)
        j = lax.broadcasted_iota(jnp.int32, (lead, cols), 1) + first_col
        acc_ref[rows:, lead:] = acc_ref[rows:, lead:] * scale + jnp.where(i == j, first, 0.0)
        i = lax.broadcasted_iota(jnp.int32, (lead, lead), 0)
        j = lax.broadcasted_iota(jnp.int32, (lead, lead), 1)
        m_ref[...] = block_ref[...] * scale + jnp.where(i == j, first, 0.0)
        invert_factor(m_ref, 64, 8)
        inverse = jnp.where(i >= j, m_ref[...], 0.0)
        highest = functools.partial(
            lax.dot_general, precision=lax.Precision.HIGHEST, preferred_element_type=jnp.float32
        )
        panel_ref[...] = highest(acc_ref[:rows, :lead], inverse, (((1,), (1,)), ((), ())))
        for c in range(0, cols, 256):
            solved = highest(inverse, acc_ref[rows:, lead + c : lead + c + 256], (((1,), (0,)), ((), ())))
            schur_ref[:, c : c + 256] = acc_ref[:rows, lead + c : lead + c + 256] - highest(
                panel_ref[...], solved, (((1,), (0,)), ((), ()))
            )


def on_device(steps, harmonic, col_scale, taps, ridge):
    params = harmonic.shape[0]
    n_epoch = lax.axis_size("epoch")
    n_row = lax.axis_size("prow")
    n_col = lax.axis_size("pcol")
    rows = params // (n_epoch * n_row)
    cols = params // n_col
    width = rows + B + cols
    epochs = steps.shape[1] * n_epoch
    count = taps.shape[0]
    tile = 512
    steps_parts = rotated(steps, "epoch")
    held = gathered_doubling(ridge, ("epoch", "prow"))
    row_of = lambda x: x.reshape(1, -1)
    in_vmem = pl.BlockSpec(memory_space=pltpu.VMEM)
    f32 = lambda *shape: jax.ShapeDtypeStruct(shape, jnp.float32)
    bf16 = lambda *shape: jax.ShapeDtypeStruct(shape, jnp.bfloat16)
    params_row, scales_row = row_of(harmonic), row_of(col_scale)
    shared = pl.pallas_call(
        functools.partial(lead_kernel, len(steps_parts)),
        out_shape=(f32(8, epochs), bf16(2 * count, count), bf16(B, epochs), f32(B, B)),
        in_specs=[in_vmem] * (len(steps_parts) + 3),
        out_specs=(in_vmem,) * 4,
        scratch_shapes=[
            pltpu.VMEM((2 * epochs // 128, 128), jnp.float32),
            pltpu.VMEM((B, 128), jnp.float32),
            pltpu.VMEM((B, count + 1024), jnp.bfloat16),
            pltpu.VMEM((B, 1024), jnp.bfloat16),
        ],
        compiler_params=pltpu.CompilerParams(vmem_limit_bytes=VMEM_LIMIT),
    )(*steps_parts, params_row, scales_row, row_of(taps))
    operands = (params_row, scales_row, row_of(ridge), held, *shared)
    return pl.pallas_call(
        functools.partial(main_kernel, (rows, B, cols, n_row)),
        grid=(epochs // (2 * tile),),
        out_shape=(f32(rows, B), f32(rows, cols)),
        in_specs=[in_vmem] * len(operands),
        out_specs=(in_vmem, in_vmem),
        scratch_shapes=[
            pltpu.VMEM((width, 128), jnp.float32),
            pltpu.VMEM((params, 128), jnp.float32),
            pltpu.VMEM((width, count + tile), jnp.bfloat16),
            pltpu.VMEM((width, tile), jnp.bfloat16),
            pltpu.VMEM((width, tile), jnp.bfloat16),
            pltpu.VMEM((rows + B, B + cols), jnp.float32),
            pltpu.VMEM((B, B), jnp.float32),
        ],
        compiler_params=pltpu.CompilerParams(vmem_limit_bytes=VMEM_LIMIT),
    )(*operands)


def solution(mesh):
    in_specs = (P(None, "epoch"), P(), P(), P(), P(("epoch", "prow")))
    out_specs = (P(("epoch", "prow"), None), P(("epoch", "prow"), "pcol"))
    return jax.shard_map(
        on_device, mesh=mesh, in_specs=in_specs, out_specs=out_specs, check_vma=False
    )
```

```python
import functools
import math

import jax
import jax.numpy as jnp
from jax import lax
from jax.experimental import pallas as pl
from jax.experimental.pallas import tpu as pltpu
from jax.sharding import PartitionSpec as P

B = 256

phase_count = 4096
SINE = (6.2831640442776635, -41.337142367123384, 81.34076873476997, -70.99343163979194)
LEAD = SINE[3]
POLY = tuple(c / LEAD for c in SINE[:3])
VMEM_LIMIT = 58 * 1024 * 1024
FACTOR_BLOCK, FACTOR_GROUP, FACTOR_PARTS = 32, 8, 4


def rotated(x, axis):
    count = lax.axis_size(axis)
    shifts = [[(i, (i + k) % count) for i in range(count)] for k in range(1, count)]
    return [x] + [lax.ppermute(x, axis, pairs) for pairs in shifts]


def split3(x):
    high = x.astype(jnp.bfloat16)
    rest = x - high.astype(jnp.float32)
    mid = rest.astype(jnp.bfloat16)
    return high, mid, (rest - mid.astype(jnp.float32)).astype(jnp.bfloat16)


def dot_f32(a, b, b_dim):
    ah, am, al = split3(a)
    bh, bm, bl = split3(b)
    return lax.dot_general(
        jnp.concatenate([ah, ah, am, ah, al, am], axis=1),
        jnp.concatenate([bh, bm, bh, bl, bh, bm], axis=b_dim),
        (((1,), (b_dim,)), ((), ())),
        preferred_element_type=jnp.float32,
    )


def factor_panel(t, first, last, group):
    row = lax.broadcasted_iota(jnp.int32, t.shape, 0)
    for j in range(first, last, group):
        span = range(group)
        cols = [jnp.broadcast_to(t[:, j + k : j + k + 1], t.shape) for k in span]
        rows = [t[j + k : j + k + 1, :] for k in span]
        pivot = [[cols[l][j + k : j + k + 1, :] for l in span] for k in span]
        done = []
        for k in span:
            root = lax.rsqrt(pivot[k][k])
            inverse = root * root
            weight = rows[k] * inverse
            for l in range(k + 1, group):
                lower = pivot[l][k]
                rows[l] = rows[l] - lower * weight
                cols[l] = cols[l] - cols[k] * (pivot[k][l] * inverse)
                for q in range(k + 1, group):
                    pivot[l][q] = pivot[l][q] - lower * (pivot[k][q] * inverse)
            t = t - jnp.where(row >= j + group, cols[k], 0.0) * weight
            done.append(rows[k] * root)
        for k in span:
            t = jnp.where(row == j + k, done[k], t)
    return t


def factor_steps(m_ref, k, size, group, parts):
    n = m_ref.shape[0]
    active = k < n // size
    here = pl.ds(pl.multiple_of(jnp.minimum(k, n // size - 1) * size, size), size)
    held = {}

    def ids(shape):
        return [lax.broadcasted_iota(jnp.int32, shape, d) for d in (0, 1)]

    def begin():
        row, lane = ids((size, 128))
        panel = m_ref[here, :]
        held["t"] = jnp.where(
            lane < size, panel[:, :128], jnp.where(lane - size == row, 1.0, 0.0)
        )

    def eliminate(first, last):
        def run():
            held["t"] = factor_panel(held["t"], first, last, group)
        return run

    def solve():
        row, lane = ids((size, 128))
        panel = m_ref[here, :]
        inverse = pltpu.roll(held["t"], 128 - size, 1)[:, :size]
        head = jnp.where(lane < size, jnp.where(lane == row, 1.0, 0.0), panel[:, :128])
        held["done"] = dot_f32(inverse, jnp.concatenate([head, panel[:, 128:]], axis=1), 0)
        low = dot_f32(m_ref[:, :size], inverse, 1)
        held["low"] = jnp.where(ids((n, size))[0] >= (k + 1) * size, low, 0.0)

    def update():
        full = m_ref[...]
        row, lane = ids((n, n))
        new = jnp.where(lane < size, 0.0, full) - dot_f32(held["low"], held["done"], 0)
        panel = m_ref[here, :]
        m_ref[...] = jnp.where(active, pltpu.roll(new, n - size, 1), full)
        m_ref[here, :] = jnp.where(active, pltpu.roll(held["done"], n - size, 1), panel)

    pieces = [begin]
    for p in range(parts):
        pieces.append(eliminate(p * size // parts, (p + 1) * size // parts))
    return pieces + [solve, update]


def fill_phases(mine, parts_refs, sums_ref, pt_ref):
    count = len(parts_refs)
    each = sums_ref.shape[0] // count
    blocks = each // 2
    for k, ref in enumerate(parts_refs):
        group = lax.rem(mine - k + count, count)
        sums_ref[pl.ds(pl.multiple_of(group * each, each), each), :] = ref[:each, :]
    total = sums_ref.shape[0]
    terms = sums_ref[...].astype(jnp.bfloat16)
    i = lax.broadcasted_iota(jnp.int32, (128, 128), 0)
    j = lax.broadcasted_iota(jnp.int32, (128, 128), 1)
    inside = jnp.dot(
        terms, jnp.where(i <= j, 1.0, 0.0).astype(jnp.bfloat16), preferred_element_type=jnp.float32
    )
    ends = jnp.dot(terms, jnp.ones((128, 128), jnp.bfloat16), preferred_element_type=jnp.float32)
    ends = ends.astype(jnp.int32)
    i = lax.broadcasted_iota(jnp.int32, (total, total), 0)
    j = lax.broadcasted_iota(jnp.int32, (total, total), 1)
    earlier = jnp.zeros((total, total), jnp.bool_)
    for track in range(2):
        mine_i = lax.rem(i, each) // blocks == track
        mine_j = lax.rem(j, each) // blocks == track
        earlier = earlier | (mine_i & mine_j & (j < i))
    earlier = jnp.where(earlier, 1.0, 0.0).astype(jnp.bfloat16)

    def before(x):
        return jnp.dot(
            earlier, x.astype(jnp.float32).astype(jnp.bfloat16), preferred_element_type=jnp.float32
        ).astype(jnp.int32)

    phase = inside.astype(jnp.int32) + before(ends & 127) + before(ends >> 7) * 128
    turn = (phase & (phase_count - 1)).astype(jnp.float32) * (1.0 / phase_count)
    pt_ref[...] = jnp.zeros_like(pt_ref)
    for r in range(total):
        group, rest = divmod(r, each)
        track, b = divmod(rest, blocks)
        lane = (group * blocks + b) * 128
        pt_ref[track : track + 1, lane : lane + 128] = turn[r : r + 1, :]


def fill_toeplitz(taps_ref, wt_ref):
    count = taps_ref.shape[1]
    taps = taps_ref[...]
    none = jnp.zeros_like(taps)
    for half, row in enumerate(([none, taps], [taps, none])):
        spread = jnp.broadcast_to(jnp.concatenate(row, axis=1), (count, 2 * count))
        spread = pltpu.roll(spread, 0, 1, stride=1, stride_axis=0)
        wt_ref[half * count : (half + 1) * count, :] = spread[:, :count].astype(jnp.bfloat16)


def parameter_table(harmonic, col_scale):
    rows = [harmonic >> 6, harmonic & 63]
    rows = [x.astype(jnp.float32) for x in rows] + [col_scale * (math.sqrt(2.0) * LEAD)]
    return jnp.concatenate(rows + [jnp.zeros((125, harmonic.shape[1]), jnp.float32)]).T


def fill_design(h_ref, pt_ref, d_ref, start, stop, lane, tile):
    here = slice(start, stop)
    p0 = pt_ref[0:1, pl.ds(tile, 256)]
    p1 = pt_ref[1:2, pl.ds(tile, 256)]
    turns = h_ref[here, 0:1] * p0 + h_ref[here, 1:2] * p1 - 0.125
    s = 0.25 - jnp.abs(turns - jnp.round(turns))
    z = s * s
    poly = ((z + POLY[2]) * z + POLY[1]) * z + POLY[0]
    d_ref[here, lane : lane + 256] = (poly * (s * h_ref[here, 2:3])).astype(jnp.bfloat16)


def fill_filtered(d_ref, wt_ref, f_ref, start, stop, block):
    count = wt_ref.shape[1]
    f_ref[start:stop, block * count : (block + 1) * count] = jnp.dot(
        d_ref[start:stop, block * count : (block + 2) * count],
        wt_ref[...],
        preferred_element_type=jnp.float32,
    ).astype(jnp.bfloat16)


def lead_kernel(n_parts, *refs):
    parts_refs = refs[:n_parts]
    harmonic_ref, scale_ref, taps_ref = refs[n_parts : n_parts + 3]
    pt_ref, wt_ref, lead_ref, block_ref = refs[n_parts + 3 : n_parts + 7]
    sums_ref, h_ref, d_ref = refs[n_parts + 7 :]
    lead, tile = lead_ref.shape
    epochs = pt_ref.shape[1]
    count = wt_ref.shape[1]
    step = pl.program_id(0)

    def design(start, block):
        for row in range(0, lead, 16):
            fill_design(
                h_ref, pt_ref, d_ref, row, row + 16, (block + 1) * count, start + block * count
            )

    @pl.when(step == 0)
    def _():
        fill_phases(lax.axis_index("epoch"), parts_refs, sums_ref, pt_ref)
        fill_toeplitz(taps_ref, wt_ref)
        h_ref[...] = parameter_table(harmonic_ref[:, :lead], scale_ref[:, :lead])
        d_ref[:, :count] = jnp.zeros((lead, count), jnp.bfloat16)
        block_ref[...] = jnp.zeros_like(block_ref)
        for b in range(tile // count):
            design(0, b)

    following = pl.multiple_of(lax.rem((step + 1) * tile, epochs), tile)
    blocks = tile // count
    for b in range(blocks):
        fill_filtered(d_ref, wt_ref, lead_ref, 0, lead, b)
        if b == min(1, blocks - 1):
            d_ref[:, :count] = d_ref[:, tile:]
        if b > 0:
            design(following, b - 1)
    design(following, blocks - 1)
    block_ref[...] += lax.dot_general(
        lead_ref[...], lead_ref[...], (((1,), (1,)), ((), ())), preferred_element_type=jnp.float32
    )


def main_kernel(shape, *refs):
    rows, lead, cols, n_row = shape
    harmonic_ref, scale_ref, ridge_ref = refs[:3]
    held_refs = refs[3 : 3 + n_row]
    pt_ref, wt_ref, lead_ref, block_ref = refs[3 + n_row : 7 + n_row]
    panel_ref, schur_ref, h_ref, r_ref, d_ref, fa_ref, fb_ref, acc_ref, m_ref, first_ref = refs[7 + n_row :]
    width, tile = fa_ref.shape
    count = wt_ref.shape[1]
    step = pl.program_id(0)
    epochs = pt_ref.shape[1]
    mine = lax.axis_index("epoch") * n_row + lax.axis_index("prow")
    first_row = pl.multiple_of(mine * rows, rows)
    first_col = pl.multiple_of(lax.axis_index("pcol") * cols, cols)
    segments = [(0, rows), (rows + lead, width)]

    def design(start, row):
        def run():
            d_ref[row : row + 16, :count] = d_ref[row : row + 16, tile:]
            for lane in range(0, tile, 256):
                fill_design(h_ref, pt_ref, d_ref, row, row + 16, count + lane, start + lane)
        return run

    def filtered(f_ref, begin, end, block):
        return lambda: fill_filtered(d_ref, wt_ref, f_ref, begin, end, block)

    def product(f_ref, begin, end, depth):
        def run():
            acc_ref[:depth, begin:end] += lax.dot_general(
                f_ref[:depth, :],
                f_ref[rows + begin : rows + end, :],
                (((1,), (1,)), ((), ())),
                preferred_element_type=jnp.float32,
            )
        return run

    def products(f_ref):
        pieces = [(0, lead, rows)]
        pieces += [(c, min(c + 256, lead + cols), rows + lead) for c in range(lead, lead + cols, 256)]
        return [product(f_ref, *piece) for piece in pieces]

    @pl.when(step == 0)
    def _():
        table = parameter_table(harmonic_ref[...], scale_ref[...])
        r_ref[...] = table
        h_ref[:rows, :] = r_ref[pl.ds(first_row, rows), :]
        h_ref[rows + lead :, :] = r_ref[pl.ds(first_col, cols), :]
        fb_ref[...] = jnp.zeros_like(fb_ref)
        acc_ref[...] = jnp.zeros_like(acc_ref)
        d_ref[...] = jnp.zeros_like(d_ref)
        n_epoch = held_refs[0].shape[0]
        first = []
        for q in range(-(-lead // rows)):
            for k, ref in enumerate(held_refs):
                group = lax.rem(lax.axis_index("prow") - k + n_row, n_row)
                block = lax.rem(lax.axis_index("epoch") - q // n_row + n_epoch, n_epoch)
                term = jnp.where(group == q % n_row, ref[pl.ds(block, 1), :rows], 0.0)
                total = term if k == 0 else total + term
            first.append(total)
        first = jnp.concatenate(first, axis=1)[:, :lead]
        first_ref[...] = jnp.concatenate([first, jnp.zeros((127, lead), jnp.float32)]).T
        i = lax.broadcasted_iota(jnp.int32, (lead, lead), 0)
        j = lax.broadcasted_iota(jnp.int32, (lead, lead), 1)
        m_ref[...] = block_ref[...] * (1.0 / epochs) + jnp.where(i == j, first_ref[:, :1], 0.0)
        for begin, end in segments:
            for row in range(begin, end, 16):
                design(0, row)()

    def phase(f_ref, before_ref, half, extra):
        following = pl.multiple_of(lax.rem((2 * step + half + 1) * tile, epochs), tile)
        f_ref[rows : rows + lead, :] = lead_ref[:, half * tile : (half + 1) * tile]
        chunk = 256
        sets = []
        for start, stop in segments:
            for at in range(start, stop, chunk):
                sets.append((at, min(at + chunk, stop)))
        later = products(before_ref)
        for k, (at, end) in enumerate(sets):
            for b in range(tile // count):
                filtered(f_ref, at, end, b)()
            for n in range(k * len(later) // len(sets), (k + 1) * len(later) // len(sets)):
                later[n]()
            for row in range(at, end, 16):
                design(following, row)()
            for n in range(k * len(extra) // len(sets), (k + 1) * len(extra) // len(sets)):
                extra[n]()

    pieces = factor_steps(m_ref, step, FACTOR_BLOCK, FACTOR_GROUP, FACTOR_PARTS)
    phase(fa_ref, fb_ref, 0, pieces[: len(pieces) // 2])
    phase(fb_ref, fa_ref, 1, pieces[len(pieces) // 2 :])

    @pl.when(step == pl.num_programs(0) - 1)
    def _():
        for run in products(fb_ref):
            run()
        mid = -(-rows // 128) * 128
        own = ridge_ref[...]
        if mid > rows:
            own = jnp.concatenate([own, jnp.zeros((1, mid - rows), jnp.float32)], axis=1)
        own = jnp.concatenate([own, jnp.zeros((127, mid), jnp.float32)]).T[:rows, :1]
        first = first_ref[:, :1]
        scale = 1.0 / epochs
        i = lax.broadcasted_iota(jnp.int32, (rows, lead + cols), 0) + first_row
        j = lax.broadcasted_iota(jnp.int32, (rows, lead + cols), 1)
        j = jnp.where(j < lead, j, j - lead + first_col)
        acc_ref[:rows, :] = acc_ref[:rows, :] * scale + jnp.where(i == j, own, 0.0)
        i = lax.broadcasted_iota(jnp.int32, (lead, cols), 0)
        j = lax.broadcasted_iota(jnp.int32, (lead, cols), 1) + first_col
        acc_ref[rows:, lead:] = acc_ref[rows:, lead:] * scale + jnp.where(i == j, first, 0.0)
        i = lax.broadcasted_iota(jnp.int32, (lead, lead), 0)
        j = lax.broadcasted_iota(jnp.int32, (lead, lead), 1)

        @pl.loop(epochs // (2 * tile), max(lead // FACTOR_BLOCK, epochs // (2 * tile)))
        def _(k):
            for run in factor_steps(m_ref, k, FACTOR_BLOCK, FACTOR_GROUP, FACTOR_PARTS):
                run()

        inverse = jnp.where(i >= j, m_ref[...], 0.0)
        highest = functools.partial(
            lax.dot_general, precision=lax.Precision.HIGHEST, preferred_element_type=jnp.float32
        )
        panel_ref[...] = highest(acc_ref[:rows, :lead], inverse, (((1,), (1,)), ((), ())))
        for c in range(0, cols, 256):
            solved = highest(inverse, acc_ref[rows:, lead + c : lead + c + 256], (((1,), (0,)), ((), ())))
            schur_ref[:, c : c + 256] = acc_ref[:rows, lead + c : lead + c + 256] - highest(
                panel_ref[...], solved, (((1,), (0,)), ((), ()))
            )


def on_device(steps, harmonic, col_scale, taps, ridge):
    params = harmonic.shape[0]
    n_epoch = lax.axis_size("epoch")
    n_row = lax.axis_size("prow")
    n_col = lax.axis_size("pcol")
    rows = params // (n_epoch * n_row)
    cols = params // n_col
    width = rows + B + cols
    epochs = steps.shape[1] * n_epoch
    count = taps.shape[0]
    tile = 512
    lead_tile = 1024
    step_rows = 2 * steps.shape[1] // 128
    ridge_rows = -(-rows // 128)
    packed = jnp.concatenate(
        [
            steps.astype(jnp.float32).reshape(step_rows, 128),
            jnp.pad(ridge, (0, ridge_rows * 128 - rows)).reshape(ridge_rows, 128),
        ]
    )
    parts = rotated(packed, "epoch")
    held = jnp.stack([x[step_rows:].reshape(-1) for x in parts])
    held = rotated(held, "prow")
    row_of = lambda x: x.reshape(1, -1)
    in_vmem = pl.BlockSpec(memory_space=pltpu.VMEM)
    f32 = lambda *shape: jax.ShapeDtypeStruct(shape, jnp.float32)
    bf16 = lambda *shape: jax.ShapeDtypeStruct(shape, jnp.bfloat16)
    params_row, scales_row = row_of(harmonic), row_of(col_scale)
    shared = pl.pallas_call(
        functools.partial(lead_kernel, len(parts)),
        grid=(epochs // lead_tile,),
        out_shape=(f32(8, epochs), bf16(2 * count, count), bf16(B, epochs), f32(B, B)),
        in_specs=[in_vmem] * (len(parts) + 3),
        out_specs=(in_vmem, in_vmem, pl.BlockSpec((B, lead_tile), lambda i: (0, i)), in_vmem),
        scratch_shapes=[
            pltpu.VMEM((2 * epochs // 128, 128), jnp.float32),
            pltpu.VMEM((B, 128), jnp.float32),
            pltpu.VMEM((B, count + lead_tile), jnp.bfloat16),
        ],
        compiler_params=pltpu.CompilerParams(vmem_limit_bytes=VMEM_LIMIT),
    )(*parts, params_row, scales_row, row_of(taps))
    operands = (params_row, scales_row, row_of(ridge), *held, *shared)
    return pl.pallas_call(
        functools.partial(main_kernel, (rows, B, cols, n_row)),
        grid=(epochs // (2 * tile),),
        out_shape=(f32(rows, B), f32(rows, cols)),
        in_specs=[in_vmem] * (len(operands) - 2)
        + [pl.BlockSpec((B, 2 * tile), lambda i: (0, i)), in_vmem],
        out_specs=(in_vmem, in_vmem),
        scratch_shapes=[
            pltpu.VMEM((width, 128), jnp.float32),
            pltpu.VMEM((params, 128), jnp.float32),
            pltpu.VMEM((width, count + tile), jnp.bfloat16),
            pltpu.VMEM((width, tile), jnp.bfloat16),
            pltpu.VMEM((width, tile), jnp.bfloat16),
            pltpu.VMEM((rows + B, B + cols), jnp.float32),
            pltpu.VMEM((B, B), jnp.float32),
            pltpu.VMEM((B, 128), jnp.float32),
        ],
        compiler_params=pltpu.CompilerParams(vmem_limit_bytes=VMEM_LIMIT),
    )(*operands)


def solution(mesh):
    in_specs = (P(None, "epoch"), P(), P(), P(), P(("epoch", "prow")))
    out_specs = (P(("epoch", "prow"), None), P(("epoch", "prow"), "pcol"))
    return jax.shard_map(
        on_device, mesh=mesh, in_specs=in_specs, out_specs=out_specs, check_vma=False
    )
```

```python
import functools
import math

import jax
import jax.numpy as jnp
from jax import lax
from jax.experimental import pallas as pl
from jax.experimental.pallas import tpu as pltpu
from jax.sharding import PartitionSpec as P

B = 256

phase_count = 4096
SINE = (6.2831640442776635, -41.337142367123384, 81.34076873476997, -70.99343163979194)
LEAD = SINE[3]
POLY = tuple(c / LEAD for c in SINE[:3])
VMEM_LIMIT = 58 * 1024 * 1024
FACTOR_BLOCK, FACTOR_GROUP, FACTOR_SLAB = 32, 4, 32


def rotated(x, axis):
    count = lax.axis_size(axis)
    shifts = [[(i, (i + k) % count) for i in range(count)] for k in range(1, count)]
    return [x] + [lax.ppermute(x, axis, pairs) for pairs in shifts]


def split3(x):
    high = x.astype(jnp.bfloat16)
    rest = x - high.astype(jnp.float32)
    mid = rest.astype(jnp.bfloat16)
    return high, mid, (rest - mid.astype(jnp.float32)).astype(jnp.bfloat16)


def dot_f32(a, b, b_dim):
    ah, am, al = split3(a)
    bh, bm, bl = split3(b)
    return lax.dot_general(
        jnp.concatenate([ah, ah, am, ah, al, am], axis=1),
        jnp.concatenate([bh, bm, bh, bl, bh, bm], axis=b_dim),
        (((1,), (b_dim,)), ((), ())),
        preferred_element_type=jnp.float32,
    )


def reciprocal(x):
    r = pl.reciprocal(x, approx=True)
    r = r * (2.0 - x * r)
    return r * (2.0 - x * r)


def factor_panel(t, size, group):
    depth = t[0].shape[0]
    row = lax.broadcasted_iota(jnp.int32, t[0].shape, 0)
    span = range(group)
    for j in range(0, size, group):
        top, at = divmod(j, depth)
        cols = [
            [jnp.broadcast_to(x[:, j + k : j + k + 1], x.shape) for x in t[top:]] for k in span
        ]
        rows = [t[top][at + k : at + k + 1, :] for k in span]
        yield
        pivot = [[cols[l][0][at + k : at + k + 1, :] for l in span] for k in span]
        done = []
        for a in range(0, group, 2):
            b = a + 1
            p, q, r = pivot[a][a], pivot[a][b], pivot[b][b]
            det = p * r - q * q
            inv = reciprocal(det)
            yield
            paa, pab, pbb = r * inv, -(q * inv), p * inv
            wa = paa * rows[a] + pab * rows[b]
            wb = pab * rows[a] + pbb * rows[b]
            for l in range(b + 1, group):
                fa = paa * pivot[a][l] + pab * pivot[b][l]
                fb = pab * pivot[a][l] + pbb * pivot[b][l]
                la, lb = pivot[l][a], pivot[l][b]
                rows[l] = rows[l] - (la * wa + lb * wb)
                cols[l] = [x - (y * fa + z * fb) for x, y, z in zip(cols[l], cols[a], cols[b])]
                for m in range(b + 1, group):
                    if m <= l:
                        ma, mb = pivot[m][a], pivot[m][b]
                        pivot[m][l] = pivot[m][l] - (ma * fa + mb * fb)
                        pivot[l][m] = pivot[m][l]
            root = lax.rsqrt(p)
            done.append(rows[a] * root)
            done.append((rows[b] - (q * root * root) * rows[a]) * lax.rsqrt(det * root * root))
            for s, (ca, cb) in enumerate(zip(cols[a], cols[b])):
                change = ca * wa + cb * wb
                if s == 0:
                    change = jnp.where(row >= at + group, change, 0.0)
                t[top + s] = t[top + s] - change
            yield
        for k in span:
            t[top] = jnp.where(row == at + k, done[k], t[top])
    return jnp.concatenate(t, axis=0) if len(t) > 1 else t[0]


def factor_step(m_ref, k, size, group):
    n = m_ref.shape[0]
    active = k < n // size
    here = pl.ds(pl.multiple_of(jnp.minimum(k, n // size - 1) * size, size), size)

    def ids(shape):
        return [lax.broadcasted_iota(jnp.int32, shape, d) for d in (0, 1)]

    row, lane = ids((size, 128))
    t = jnp.where(lane < size, m_ref[here, :128], jnp.where(lane - size == row, 1.0, 0.0))
    t = yield from factor_panel(
        [t[r : r + FACTOR_SLAB, :] for r in range(0, size, FACTOR_SLAB)], size, group
    )
    yield
    panel = m_ref[here, :]
    inverse = pltpu.roll(t, 128 - size, 1)[:, :size]
    head = jnp.where(lane < size, jnp.where(lane == row, 1.0, 0.0), panel[:, :128])
    yield
    done = dot_f32(inverse, jnp.concatenate([head, panel[:, 128:]], axis=1), 0)
    yield
    low = dot_f32(m_ref[:, :size], inverse, 1)
    yield
    low = jnp.where(ids((n, size))[0] >= (k + 1) * size, low, 0.0)
    change = dot_f32(low, done, 0)
    for r in range(0, n, 32):
        yield
        full = m_ref[r : r + 32, :]
        new = jnp.where(ids((32, n))[1] < size, 0.0, full) - change[r : r + 32, :]
        m_ref[r : r + 32, :] = jnp.where(active, pltpu.roll(new, n - size, 1), full)
    yield
    m_ref[here, :] = jnp.where(active, pltpu.roll(done, n - size, 1), panel)


def fill_phases(mine, parts_refs, sums_ref, pt_ref):
    count = len(parts_refs)
    each = sums_ref.shape[0] // count
    blocks = each // 2
    for k, ref in enumerate(parts_refs):
        group = lax.rem(mine - k + count, count)
        sums_ref[pl.ds(pl.multiple_of(group * each, each), each), :] = ref[:each, :]
    total = sums_ref.shape[0]
    terms = sums_ref[...].astype(jnp.bfloat16)
    i = lax.broadcasted_iota(jnp.int32, (128, 128), 0)
    j = lax.broadcasted_iota(jnp.int32, (128, 128), 1)
    inside = jnp.dot(
        terms, jnp.where(i <= j, 1.0, 0.0).astype(jnp.bfloat16), preferred_element_type=jnp.float32
    )
    ends = jnp.dot(terms, jnp.ones((128, 128), jnp.bfloat16), preferred_element_type=jnp.float32)
    ends = ends.astype(jnp.int32)
    i = lax.broadcasted_iota(jnp.int32, (total, total), 0)
    j = lax.broadcasted_iota(jnp.int32, (total, total), 1)
    earlier = jnp.zeros((total, total), jnp.bool_)
    for track in range(2):
        mine_i = lax.rem(i, each) // blocks == track
        mine_j = lax.rem(j, each) // blocks == track
        earlier = earlier | (mine_i & mine_j & (j < i))
    earlier = jnp.where(earlier, 1.0, 0.0).astype(jnp.bfloat16)

    def before(x):
        return jnp.dot(
            earlier, x.astype(jnp.float32).astype(jnp.bfloat16), preferred_element_type=jnp.float32
        ).astype(jnp.int32)

    phase = inside.astype(jnp.int32) + before(ends & 127) + before(ends >> 7) * 128
    turn = (phase & (phase_count - 1)).astype(jnp.float32) * (1.0 / phase_count)
    pt_ref[...] = jnp.zeros_like(pt_ref)
    for r in range(total):
        group, rest = divmod(r, each)
        track, b = divmod(rest, blocks)
        lane = (group * blocks + b) * 128
        pt_ref[track : track + 1, lane : lane + 128] = turn[r : r + 1, :]


def fill_toeplitz(taps_ref, wt_ref):
    count = taps_ref.shape[1]
    taps = taps_ref[...]
    none = jnp.zeros_like(taps)
    for half, row in enumerate(([none, taps], [taps, none])):
        spread = jnp.broadcast_to(jnp.concatenate(row, axis=1), (count, 2 * count))
        spread = pltpu.roll(spread, 0, 1, stride=1, stride_axis=0)
        wt_ref[half * count : (half + 1) * count, :] = spread[:, :count].astype(jnp.bfloat16)


def parameter_table(harmonic, col_scale):
    rows = [harmonic >> 6, harmonic & 63]
    rows = [x.astype(jnp.float32) for x in rows] + [col_scale * (math.sqrt(2.0) * LEAD)]
    return jnp.concatenate(rows + [jnp.zeros((125, harmonic.shape[1]), jnp.float32)]).T


def fill_design(h_ref, pt_ref, d_ref, start, stop, lane, tile):
    here = slice(start, stop)
    p0 = pt_ref[0:1, pl.ds(tile, 256)]
    p1 = pt_ref[1:2, pl.ds(tile, 256)]
    turns = h_ref[here, 0:1] * p0 + h_ref[here, 1:2] * p1 - 0.125
    s = 0.25 - jnp.abs(turns - jnp.round(turns))
    z = s * s
    poly = ((z + POLY[2]) * z + POLY[1]) * z + POLY[0]
    d_ref[here, lane : lane + 256] = (poly * (s * h_ref[here, 2:3])).astype(jnp.bfloat16)


def fill_filtered(d_ref, wt_ref, f_ref, start, stop, block):
    count = wt_ref.shape[1]
    f_ref[start:stop, block * count : (block + 1) * count] = jnp.dot(
        d_ref[start:stop, block * count : (block + 2) * count],
        wt_ref[...],
        preferred_element_type=jnp.float32,
    ).astype(jnp.bfloat16)


def lead_kernel(n_parts, *refs):
    parts_refs = refs[:n_parts]
    harmonic_ref, scale_ref, taps_ref = refs[n_parts : n_parts + 3]
    pt_ref, wt_ref, lead_ref, block_ref = refs[n_parts + 3 : n_parts + 7]
    sums_ref, h_ref, d_ref = refs[n_parts + 7 :]
    lead, tile = lead_ref.shape
    epochs = pt_ref.shape[1]
    count = wt_ref.shape[1]
    step = pl.program_id(0)

    def design(start, block):
        for row in range(0, lead, 16):
            fill_design(
                h_ref, pt_ref, d_ref, row, row + 16, (block + 1) * count, start + block * count
            )

    @pl.when(step == 0)
    def _():
        fill_phases(lax.axis_index("epoch"), parts_refs, sums_ref, pt_ref)
        fill_toeplitz(taps_ref, wt_ref)
        h_ref[...] = parameter_table(harmonic_ref[:, :lead], scale_ref[:, :lead])
        d_ref[:, :count] = jnp.zeros((lead, count), jnp.bfloat16)
        block_ref[...] = jnp.zeros_like(block_ref)
        for b in range(tile // count):
            design(0, b)

    following = pl.multiple_of(lax.rem((step + 1) * tile, epochs), tile)
    blocks = tile // count
    for b in range(blocks):
        fill_filtered(d_ref, wt_ref, lead_ref, 0, lead, b)
        if b == min(1, blocks - 1):
            d_ref[:, :count] = d_ref[:, tile:]
        if b > 0:
            design(following, b - 1)
    design(following, blocks - 1)
    block_ref[...] += lax.dot_general(
        lead_ref[...], lead_ref[...], (((1,), (1,)), ((), ())), preferred_element_type=jnp.float32
    )


def main_kernel(shape, *refs):
    rows, lead, cols, n_row = shape
    harmonic_ref, scale_ref, ridge_ref = refs[:3]
    held_refs = refs[3 : 3 + n_row]
    pt_ref, wt_ref, lead_ref, block_ref = refs[3 + n_row : 7 + n_row]
    panel_ref, schur_ref, h_ref, r_ref, d_ref, fa_ref, fb_ref, acc_ref, m_ref, first_ref = refs[7 + n_row :]
    width, tile = fa_ref.shape
    count = wt_ref.shape[1]
    step = pl.program_id(0)
    epochs = pt_ref.shape[1]
    mine = lax.axis_index("epoch") * n_row + lax.axis_index("prow")
    first_row = pl.multiple_of(mine * rows, rows)
    first_col = pl.multiple_of(lax.axis_index("pcol") * cols, cols)
    segments = [(0, rows), (rows + lead, width)]
    chunks = [(at, min(at + 256, stop)) for start, stop in segments for at in range(start, stop, 256)]
    n_lead_chunks = -(-rows // 256)

    def design(start, row):
        def run():
            d_ref[row : row + 16, :count] = d_ref[row : row + 16, tile:]
            for lane in range(0, tile, 256):
                fill_design(h_ref, pt_ref, d_ref, row, row + 16, count + lane, start + lane)
        return run

    def filtered(f_ref, begin, end, block):
        return lambda: fill_filtered(d_ref, wt_ref, f_ref, begin, end, block)

    def product(f_ref, begin, end, depth):
        def run():
            acc_ref[:depth, begin:end] += lax.dot_general(
                f_ref[:depth, :],
                f_ref[rows + begin : rows + end, :],
                (((1,), (1,)), ((), ())),
                preferred_element_type=jnp.float32,
            )
        return run

    def products(f_ref):
        pieces = [(0, lead, rows)]
        pieces += [(c, min(c + 256, lead + cols), rows + lead) for c in range(lead, lead + cols, 256)]
        return [(product(f_ref, *p), (p[1] - p[0]) * p[2] * tile) for p in pieces]

    @pl.when(step == 0)
    def _():
        table = parameter_table(harmonic_ref[...], scale_ref[...])
        r_ref[...] = table
        h_ref[:rows, :] = r_ref[pl.ds(first_row, rows), :]
        h_ref[rows + lead :, :] = r_ref[pl.ds(first_col, cols), :]
        acc_ref[...] = jnp.zeros_like(acc_ref)
        d_ref[...] = jnp.zeros_like(d_ref)
        n_epoch = held_refs[0].shape[0]
        first = []
        for q in range(-(-lead // rows)):
            for k, ref in enumerate(held_refs):
                group = lax.rem(lax.axis_index("prow") - k + n_row, n_row)
                block = lax.rem(lax.axis_index("epoch") - q // n_row + n_epoch, n_epoch)
                term = jnp.where(group == q % n_row, ref[pl.ds(block, 1), :rows], 0.0)
                total = term if k == 0 else total + term
            first.append(total)
        first = jnp.concatenate(first, axis=1)[:, :lead]
        first_ref[...] = jnp.concatenate([first, jnp.zeros((127, lead), jnp.float32)]).T
        i = lax.broadcasted_iota(jnp.int32, (lead, lead), 0)
        j = lax.broadcasted_iota(jnp.int32, (lead, lead), 1)
        m_ref[...] = block_ref[...] * (1.0 / epochs) + jnp.where(i == j, first_ref[:, :1], 0.0)
        for begin, end in segments:
            for row in range(begin, end, 16):
                design(0, row)()

    def phase(f_ref, half, extra):
        following = pl.multiple_of(lax.rem((2 * step + half + 1) * tile, epochs), tile)
        f_ref[rows : rows + lead, :] = lead_ref[:, half * tile : (half + 1) * tile]
        work, ready = [], []

        def filters(begin, end):
            for b in range(tile // count):
                work.append((filtered(f_ref, begin, end, b), (end - begin) * 2 * count * count, None))
            work[-1] = (*work[-1][:2], range(begin, end, 16))

        pieces = products(f_ref)
        for begin, end in chunks[:n_lead_chunks]:
            filters(begin, end)
        for n, (begin, end) in enumerate(chunks[n_lead_chunks:]):
            filters(begin, end)
            work.append((*pieces[n], None))
        for piece in pieces[len(chunks) - n_lead_chunks :]:
            work.append((*piece, None))
        total, spent, given = sum(w[1] for w in work), 0, 0
        every = sum(end - begin for begin, end in chunks) // 16
        for run, cost, rows_done in work:
            run()
            spent += cost
            ready += list(rows_done or ())
            while given < every * spent // total and ready:
                design(following, ready.pop(0))()
                next(extra, None)
                given += 1
        for row in ready:
            design(following, row)()
            next(extra, None)

    factor = factor_step(m_ref, step, FACTOR_BLOCK, FACTOR_GROUP)
    phase(fa_ref, 0, factor)
    phase(fb_ref, 1, factor)
    for _ in factor:
        pass

    @pl.when(step == pl.num_programs(0) - 1)
    def _():
        mid = -(-rows // 128) * 128
        own = ridge_ref[...]
        if mid > rows:
            own = jnp.concatenate([own, jnp.zeros((1, mid - rows), jnp.float32)], axis=1)
        own = jnp.concatenate([own, jnp.zeros((127, mid), jnp.float32)]).T[:rows, :1]
        first = first_ref[:, :1]
        scale = 1.0 / epochs
        i = lax.broadcasted_iota(jnp.int32, (rows, lead + cols), 0) + first_row
        j = lax.broadcasted_iota(jnp.int32, (rows, lead + cols), 1)
        j = jnp.where(j < lead, j, j - lead + first_col)
        acc_ref[:rows, :] = acc_ref[:rows, :] * scale + jnp.where(i == j, own, 0.0)
        i = lax.broadcasted_iota(jnp.int32, (lead, cols), 0)
        j = lax.broadcasted_iota(jnp.int32, (lead, cols), 1) + first_col
        acc_ref[rows:, lead:] = acc_ref[rows:, lead:] * scale + jnp.where(i == j, first, 0.0)
        i = lax.broadcasted_iota(jnp.int32, (lead, lead), 0)
        j = lax.broadcasted_iota(jnp.int32, (lead, lead), 1)

        @pl.loop(epochs // (2 * tile), max(lead // FACTOR_BLOCK, epochs // (2 * tile)))
        def _(k):
            for _ in factor_step(m_ref, k, FACTOR_BLOCK, FACTOR_GROUP):
                pass

        inverse = jnp.where(i >= j, m_ref[...], 0.0)
        highest = functools.partial(
            lax.dot_general, precision=lax.Precision.HIGHEST, preferred_element_type=jnp.float32
        )
        panel_ref[...] = highest(acc_ref[:rows, :lead], inverse, (((1,), (1,)), ((), ())))
        for c in range(0, cols, 256):
            solved = highest(inverse, acc_ref[rows:, lead + c : lead + c + 256], (((1,), (0,)), ((), ())))
            schur_ref[:, c : c + 256] = acc_ref[:rows, lead + c : lead + c + 256] - highest(
                panel_ref[...], solved, (((1,), (0,)), ((), ()))
            )


def on_device(steps, harmonic, col_scale, taps, ridge):
    params = harmonic.shape[0]
    n_epoch = lax.axis_size("epoch")
    n_row = lax.axis_size("prow")
    n_col = lax.axis_size("pcol")
    rows = params // (n_epoch * n_row)
    cols = params // n_col
    width = rows + B + cols
    epochs = steps.shape[1] * n_epoch
    count = taps.shape[0]
    tile = 512
    lead_tile = 1024
    step_rows = 2 * steps.shape[1] // 128
    ridge_rows = -(-rows // 128)
    packed = jnp.concatenate(
        [
            steps.astype(jnp.float32).reshape(step_rows, 128),
            jnp.pad(ridge, (0, ridge_rows * 128 - rows)).reshape(ridge_rows, 128),
        ]
    )
    parts = rotated(packed, "epoch")
    held = jnp.stack([x[step_rows:].reshape(-1) for x in parts])
    held = rotated(held, "prow")
    row_of = lambda x: x.reshape(1, -1)
    in_vmem = pl.BlockSpec(memory_space=pltpu.VMEM)
    f32 = lambda *shape: jax.ShapeDtypeStruct(shape, jnp.float32)
    bf16 = lambda *shape: jax.ShapeDtypeStruct(shape, jnp.bfloat16)
    params_row, scales_row = row_of(harmonic), row_of(col_scale)
    shared = pl.pallas_call(
        functools.partial(lead_kernel, len(parts)),
        grid=(epochs // lead_tile,),
        out_shape=(f32(8, epochs), bf16(2 * count, count), bf16(B, epochs), f32(B, B)),
        in_specs=[in_vmem] * (len(parts) + 3),
        out_specs=(in_vmem, in_vmem, pl.BlockSpec((B, lead_tile), lambda i: (0, i)), in_vmem),
        scratch_shapes=[
            pltpu.VMEM((2 * epochs // 128, 128), jnp.float32),
            pltpu.VMEM((B, 128), jnp.float32),
            pltpu.VMEM((B, count + lead_tile), jnp.bfloat16),
        ],
        compiler_params=pltpu.CompilerParams(vmem_limit_bytes=VMEM_LIMIT),
    )(*parts, params_row, scales_row, row_of(taps))
    operands = (params_row, scales_row, row_of(ridge), *held, *shared)
    return pl.pallas_call(
        functools.partial(main_kernel, (rows, B, cols, n_row)),
        grid=(epochs // (2 * tile),),
        out_shape=(f32(rows, B), f32(rows, cols)),
        in_specs=[in_vmem] * (len(operands) - 2)
        + [pl.BlockSpec((B, 2 * tile), lambda i: (0, i)), in_vmem],
        out_specs=(in_vmem, in_vmem),
        scratch_shapes=[
            pltpu.VMEM((width, 128), jnp.float32),
            pltpu.VMEM((params, 128), jnp.float32),
            pltpu.VMEM((width, count + tile), jnp.bfloat16),
            pltpu.VMEM((width, tile), jnp.bfloat16),
            pltpu.VMEM((width, tile), jnp.bfloat16),
            pltpu.VMEM((rows + B, B + cols), jnp.float32),
            pltpu.VMEM((B, B), jnp.float32),
            pltpu.VMEM((B, 128), jnp.float32),
        ],
        compiler_params=pltpu.CompilerParams(vmem_limit_bytes=VMEM_LIMIT),
    )(*operands)


def solution(mesh):
    in_specs = (P(None, "epoch"), P(), P(), P(), P(("epoch", "prow")))
    out_specs = (P(("epoch", "prow"), None), P(("epoch", "prow"), "pcol"))
    return jax.shard_map(
        on_device, mesh=mesh, in_specs=in_specs, out_specs=out_specs, check_vma=False
    )
```

```python
import functools
import math

import jax
import jax.numpy as jnp
from jax import lax
from jax.experimental import pallas as pl
from jax.experimental.pallas import tpu as pltpu
from jax.sharding import PartitionSpec as P

B = 256

phase_count = 4096
SINE = (6.2831640442776635, -41.337142367123384, 81.34076873476997, -70.99343163979194)
LEAD = SINE[3]
POLY = tuple(c / LEAD for c in SINE[:3])
VMEM_LIMIT = 58 * 1024 * 1024
FACTOR_BLOCK, FACTOR_GROUP, FACTOR_SLAB = 32, 4, 32


def rotated(x, axis):
    count = lax.axis_size(axis)
    shifts = [[(i, (i + k) % count) for i in range(count)] for k in range(1, count)]
    return [x] + [lax.ppermute(x, axis, pairs) for pairs in shifts]


def split3(x):
    high = x.astype(jnp.bfloat16)
    rest = x - high.astype(jnp.float32)
    mid = rest.astype(jnp.bfloat16)
    return high, mid, (rest - mid.astype(jnp.float32)).astype(jnp.bfloat16)


def dot_f32(a, b, b_dim):
    ah, am, al = split3(a)
    bh, bm, bl = split3(b)
    return lax.dot_general(
        jnp.concatenate([ah, ah, am, ah, al, am], axis=1),
        jnp.concatenate([bh, bm, bh, bl, bh, bm], axis=b_dim),
        (((1,), (b_dim,)), ((), ())),
        preferred_element_type=jnp.float32,
    )


def reciprocal(x):
    r = pl.reciprocal(x, approx=True)
    r = r * (2.0 - x * r)
    return r * (2.0 - x * r)


def factor_panel(t, size, group):
    depth = t[0].shape[0]
    row = lax.broadcasted_iota(jnp.int32, t[0].shape, 0)
    span = range(group)
    for j in range(0, size, group):
        top, at = divmod(j, depth)
        cols = [
            [jnp.broadcast_to(x[:, j + k : j + k + 1], x.shape) for x in t[top:]] for k in span
        ]
        rows = [t[top][at + k : at + k + 1, :] for k in span]
        yield
        pivot = [[cols[l][0][at + k : at + k + 1, :] for l in span] for k in span]
        done = []
        for a in range(0, group, 2):
            b = a + 1
            p, q, r = pivot[a][a], pivot[a][b], pivot[b][b]
            det = p * r - q * q
            inv = reciprocal(det)
            yield
            paa, pab, pbb = r * inv, -(q * inv), p * inv
            wa = paa * rows[a] + pab * rows[b]
            wb = pab * rows[a] + pbb * rows[b]
            for l in range(b + 1, group):
                fa = paa * pivot[a][l] + pab * pivot[b][l]
                fb = pab * pivot[a][l] + pbb * pivot[b][l]
                la, lb = pivot[l][a], pivot[l][b]
                rows[l] = rows[l] - (la * wa + lb * wb)
                cols[l] = [x - (y * fa + z * fb) for x, y, z in zip(cols[l], cols[a], cols[b])]
                for m in range(b + 1, group):
                    if m <= l:
                        ma, mb = pivot[m][a], pivot[m][b]
                        pivot[m][l] = pivot[m][l] - (ma * fa + mb * fb)
                        pivot[l][m] = pivot[m][l]
            root = lax.rsqrt(p)
            done.append(rows[a] * root)
            done.append((rows[b] - (q * root * root) * rows[a]) * lax.rsqrt(det * root * root))
            for s, (ca, cb) in enumerate(zip(cols[a], cols[b])):
                change = ca * wa + cb * wb
                if s == 0:
                    change = jnp.where(row >= at + group, change, 0.0)
                t[top + s] = t[top + s] - change
            yield
        for k in span:
            t[top] = jnp.where(row == at + k, done[k], t[top])
    return jnp.concatenate(t, axis=0) if len(t) > 1 else t[0]


def factor_step(m_ref, k, size, group):
    n = m_ref.shape[0]
    active = k < n // size
    here = pl.ds(pl.multiple_of(jnp.minimum(k, n // size - 1) * size, size), size)

    def ids(shape):
        return [lax.broadcasted_iota(jnp.int32, shape, d) for d in (0, 1)]

    row, lane = ids((size, 128))
    t = jnp.where(lane < size, m_ref[here, :128], jnp.where(lane - size == row, 1.0, 0.0))
    t = yield from factor_panel(
        [t[r : r + FACTOR_SLAB, :] for r in range(0, size, FACTOR_SLAB)], size, group
    )
    yield
    panel = m_ref[here, :]
    inverse = pltpu.roll(t, 128 - size, 1)[:, :size]
    head = jnp.where(lane < size, jnp.where(lane == row, 1.0, 0.0), panel[:, :128])
    yield
    done = dot_f32(inverse, jnp.concatenate([head, panel[:, 128:]], axis=1), 0)
    yield
    low = dot_f32(m_ref[:, :size], inverse, 1)
    yield
    low = jnp.where(ids((n, size))[0] >= (k + 1) * size, low, 0.0)
    change = dot_f32(low, done, 0)
    for r in range(0, n, 32):
        yield
        full = m_ref[r : r + 32, :]
        new = jnp.where(ids((32, n))[1] < size, 0.0, full) - change[r : r + 32, :]
        m_ref[r : r + 32, :] = jnp.where(active, pltpu.roll(new, n - size, 1), full)
    yield
    m_ref[here, :] = jnp.where(active, pltpu.roll(done, n - size, 1), panel)


def fill_phases(mine, parts_refs, sums_ref, pt_ref):
    count = len(parts_refs)
    each = sums_ref.shape[0] // count
    blocks = each // 2
    for k, ref in enumerate(parts_refs):
        group = lax.rem(mine - k + count, count)
        lanes = [ref[a : a + 1, b * 128 : (b + 1) * 128] for a in range(2) for b in range(blocks)]
        rows = pl.ds(pl.multiple_of(group * each, each), each)
        sums_ref[rows, :] = jnp.concatenate(lanes, axis=0)
    total = sums_ref.shape[0]
    terms = sums_ref[...].astype(jnp.bfloat16)
    i = lax.broadcasted_iota(jnp.int32, (128, 128), 0)
    j = lax.broadcasted_iota(jnp.int32, (128, 128), 1)
    inside = jnp.dot(
        terms, jnp.where(i <= j, 1.0, 0.0).astype(jnp.bfloat16), preferred_element_type=jnp.float32
    )
    ends = jnp.dot(terms, jnp.ones((128, 128), jnp.bfloat16), preferred_element_type=jnp.float32)
    ends = ends.astype(jnp.int32)
    i = lax.broadcasted_iota(jnp.int32, (total, total), 0)
    j = lax.broadcasted_iota(jnp.int32, (total, total), 1)
    earlier = jnp.zeros((total, total), jnp.bool_)
    for track in range(2):
        mine_i = lax.rem(i, each) // blocks == track
        mine_j = lax.rem(j, each) // blocks == track
        earlier = earlier | (mine_i & mine_j & (j < i))
    earlier = jnp.where(earlier, 1.0, 0.0).astype(jnp.bfloat16)

    def before(x):
        return jnp.dot(
            earlier, x.astype(jnp.float32).astype(jnp.bfloat16), preferred_element_type=jnp.float32
        ).astype(jnp.int32)

    phase = inside.astype(jnp.int32) + before(ends & 127) + before(ends >> 7) * 128
    turn = (phase & (phase_count - 1)).astype(jnp.float32) * (1.0 / phase_count)
    pt_ref[...] = jnp.zeros_like(pt_ref)
    for r in range(total):
        group, rest = divmod(r, each)
        track, b = divmod(rest, blocks)
        lane = (group * blocks + b) * 128
        pt_ref[track : track + 1, lane : lane + 128] = turn[r : r + 1, :]


def fill_toeplitz(taps_ref, wt_ref):
    count = taps_ref.shape[1]
    taps = taps_ref[...]
    none = jnp.zeros_like(taps)
    for half, row in enumerate(([none, taps], [taps, none])):
        spread = jnp.broadcast_to(jnp.concatenate(row, axis=1), (count, 2 * count))
        spread = pltpu.roll(spread, 0, 1, stride=1, stride_axis=0)
        wt_ref[half * count : (half + 1) * count, :] = spread[:, :count].astype(jnp.bfloat16)


def parameter_table(harmonic, col_scale):
    rows = [harmonic >> 6, harmonic & 63]
    rows = [x.astype(jnp.float32) for x in rows] + [col_scale * (math.sqrt(2.0) * LEAD)]
    return jnp.concatenate(rows + [jnp.zeros((125, harmonic.shape[1]), jnp.float32)]).T


def fill_design(h_ref, pt_ref, d_ref, start, stop, lane, tile):
    here = slice(start, stop)
    p0 = pt_ref[0:1, pl.ds(tile, 256)]
    p1 = pt_ref[1:2, pl.ds(tile, 256)]
    turns = h_ref[here, 0:1] * p0 + h_ref[here, 1:2] * p1 - 0.125
    s = 0.25 - jnp.abs(turns - jnp.round(turns))
    z = s * s
    poly = ((z + POLY[2]) * z + POLY[1]) * z + POLY[0]
    d_ref[here, lane : lane + 256] = (poly * (s * h_ref[here, 2:3])).astype(jnp.bfloat16)


def fill_filtered(d_ref, wt_ref, f_ref, start, stop, block):
    count = wt_ref.shape[1]
    f_ref[start:stop, block * count : (block + 1) * count] = jnp.dot(
        d_ref[start:stop, block * count : (block + 2) * count],
        wt_ref[...],
        preferred_element_type=jnp.float32,
    ).astype(jnp.bfloat16)


def fill_lead(h_ref, pt_ref, wt_ref, d_ref, lead_ref, block_ref):
    tiles, lead, tile = lead_ref.shape
    epochs = pt_ref.shape[1]
    count = wt_ref.shape[1]
    blocks = tile // count
    d_ref[:, :count] = jnp.zeros((lead, count), jnp.bfloat16)
    block_ref[...] = jnp.zeros_like(block_ref)

    def design(start, block):
        for row in range(0, lead, 16):
            fill_design(
                h_ref, pt_ref, d_ref, row, row + 16, (block + 1) * count, start + block * count
            )

    for b in range(blocks):
        design(0, b)

    @pl.loop(0, tiles)
    def _(step):
        following = pl.multiple_of(lax.rem((step + 1) * tile, epochs), tile)
        out_ref = lead_ref.at[step]
        for b in range(blocks):
            fill_filtered(d_ref, wt_ref, out_ref, 0, lead, b)
            if b == min(1, blocks - 1):
                d_ref[:, :count] = d_ref[:, tile:]
            if b > 0:
                design(following, b - 1)
        design(following, blocks - 1)
        block_ref[...] += lax.dot_general(
            out_ref[...], out_ref[...], (((1,), (1,)), ((), ())), preferred_element_type=jnp.float32
        )


def main_kernel(shape, *refs):
    rows, lead, cols, n_epoch, n_row = shape
    parts_refs, refs = refs[:n_epoch], refs[n_epoch:]
    held_refs, refs = refs[:n_row], refs[n_row:]
    harmonic_ref, scale_ref, taps_ref, ridge_ref, panel_ref, schur_ref = refs[:6]
    sums_ref, pt_ref, wt_ref, dl_ref, lead_ref, block_ref = refs[6:12]
    h_ref, r_ref, d_ref, fa_ref, fb_ref, acc_ref, m_ref, first_ref = refs[12:]
    width, tile = fa_ref.shape
    count = wt_ref.shape[1]
    step = pl.program_id(0)
    epochs = pt_ref.shape[1]
    mine = lax.axis_index("epoch") * n_row + lax.axis_index("prow")
    first_row = pl.multiple_of(mine * rows, rows)
    first_col = pl.multiple_of(lax.axis_index("pcol") * cols, cols)
    segments = [(0, rows), (rows + lead, width)]
    chunks = [(at, min(at + 256, stop)) for start, stop in segments for at in range(start, stop, 256)]
    n_lead_chunks = -(-rows // 256)

    def design(start, row):
        def run():
            d_ref[row : row + 16, :count] = d_ref[row : row + 16, tile:]
            for lane in range(0, tile, 256):
                fill_design(h_ref, pt_ref, d_ref, row, row + 16, count + lane, start + lane)
        return run

    def filtered(f_ref, begin, end, block):
        return lambda: fill_filtered(d_ref, wt_ref, f_ref, begin, end, block)

    def product(f_ref, begin, end, depth):
        def run():
            acc_ref[:depth, begin:end] += lax.dot_general(
                f_ref[:depth, :],
                f_ref[rows + begin : rows + end, :],
                (((1,), (1,)), ((), ())),
                preferred_element_type=jnp.float32,
            )
        return run

    def products(f_ref):
        pieces = [(0, lead, rows)]
        pieces += [(c, min(c + 256, lead + cols), rows + lead) for c in range(lead, lead + cols, 256)]
        return [(product(f_ref, *p), (p[1] - p[0]) * p[2] * tile) for p in pieces]

    @pl.when(step == 0)
    def _():
        fill_phases(lax.axis_index("epoch"), parts_refs, sums_ref, pt_ref)
        fill_toeplitz(taps_ref, wt_ref)
        r_ref[...] = parameter_table(harmonic_ref[...], scale_ref[...])
        fill_lead(r_ref, pt_ref, wt_ref, dl_ref, lead_ref, block_ref)
        h_ref[:rows, :] = r_ref[pl.ds(first_row, rows), :]
        h_ref[rows + lead :, :] = r_ref[pl.ds(first_col, cols), :]
        acc_ref[...] = jnp.zeros_like(acc_ref)
        d_ref[...] = jnp.zeros_like(d_ref)
        first = []
        for q in range(-(-lead // rows)):
            for k, ref in enumerate(held_refs):
                group = lax.rem(lax.axis_index("prow") - k + n_row, n_row)
                block = lax.rem(lax.axis_index("epoch") - q // n_row + n_epoch, n_epoch)
                term = jnp.where(group == q % n_row, ref[pl.ds(block, 1), :rows], 0.0)
                total = term if k == 0 else total + term
            first.append(total)
        first = jnp.concatenate(first, axis=1)[:, :lead]
        first_ref[...] = jnp.concatenate([first, jnp.zeros((127, lead), jnp.float32)]).T
        i = lax.broadcasted_iota(jnp.int32, (lead, lead), 0)
        j = lax.broadcasted_iota(jnp.int32, (lead, lead), 1)
        m_ref[...] = block_ref[...] * (1.0 / epochs) + jnp.where(i == j, first_ref[:, :1], 0.0)
        for begin, end in segments:
            for row in range(begin, end, 16):
                design(0, row)()

    def phase(f_ref, half, extra):
        following = pl.multiple_of(lax.rem((2 * step + half + 1) * tile, epochs), tile)
        f_ref[rows : rows + lead, :] = lead_ref[step, :, half * tile : (half + 1) * tile]
        work, ready = [], []

        def filters(begin, end):
            for b in range(tile // count):
                work.append((filtered(f_ref, begin, end, b), (end - begin) * 2 * count * count, None))
            work[-1] = (*work[-1][:2], range(begin, end, 16))

        pieces = products(f_ref)
        for begin, end in chunks[:n_lead_chunks]:
            filters(begin, end)
        for n, (begin, end) in enumerate(chunks[n_lead_chunks:]):
            filters(begin, end)
            work.append((*pieces[n], None))
        for piece in pieces[len(chunks) - n_lead_chunks :]:
            work.append((*piece, None))
        total, spent, given = sum(w[1] for w in work), 0, 0
        every = sum(end - begin for begin, end in chunks) // 16
        for run, cost, rows_done in work:
            run()
            spent += cost
            ready += list(rows_done or ())
            while given < every * spent // total and ready:
                design(following, ready.pop(0))()
                next(extra, None)
                given += 1
        for row in ready:
            design(following, row)()
            next(extra, None)

    factor = factor_step(m_ref, step, FACTOR_BLOCK, FACTOR_GROUP)
    phase(fa_ref, 0, factor)
    phase(fb_ref, 1, factor)
    for _ in factor:
        pass

    @pl.when(step == pl.num_programs(0) - 1)
    def _():
        mid = -(-rows // 128) * 128
        own = ridge_ref[...]
        if mid > rows:
            own = jnp.concatenate([own, jnp.zeros((1, mid - rows), jnp.float32)], axis=1)
        own = jnp.concatenate([own, jnp.zeros((127, mid), jnp.float32)]).T[:rows, :1]
        first = first_ref[:, :1]
        scale = 1.0 / epochs
        i = lax.broadcasted_iota(jnp.int32, (rows, lead + cols), 0) + first_row
        j = lax.broadcasted_iota(jnp.int32, (rows, lead + cols), 1)
        j = jnp.where(j < lead, j, j - lead + first_col)
        acc_ref[:rows, :] = acc_ref[:rows, :] * scale + jnp.where(i == j, own, 0.0)
        i = lax.broadcasted_iota(jnp.int32, (lead, cols), 0)
        j = lax.broadcasted_iota(jnp.int32, (lead, cols), 1) + first_col
        acc_ref[rows:, lead:] = acc_ref[rows:, lead:] * scale + jnp.where(i == j, first, 0.0)
        i = lax.broadcasted_iota(jnp.int32, (lead, lead), 0)
        j = lax.broadcasted_iota(jnp.int32, (lead, lead), 1)

        @pl.loop(epochs // (2 * tile), max(lead // FACTOR_BLOCK, epochs // (2 * tile)))
        def _(k):
            for _ in factor_step(m_ref, k, FACTOR_BLOCK, FACTOR_GROUP):
                pass

        inverse = jnp.where(i >= j, m_ref[...], 0.0)
        highest = functools.partial(
            lax.dot_general, precision=lax.Precision.HIGHEST, preferred_element_type=jnp.float32
        )
        panel_ref[...] = highest(acc_ref[:rows, :lead], inverse, (((1,), (1,)), ((), ())))
        for c in range(0, cols, 256):
            solved = highest(inverse, acc_ref[rows:, lead + c : lead + c + 256], (((1,), (0,)), ((), ())))
            schur_ref[:, c : c + 256] = acc_ref[:rows, lead + c : lead + c + 256] - highest(
                panel_ref[...], solved, (((1,), (0,)), ((), ()))
            )


def on_device(steps, harmonic, col_scale, taps, ridge):
    params = harmonic.shape[0]
    n_epoch = lax.axis_size("epoch")
    n_row = lax.axis_size("prow")
    n_col = lax.axis_size("pcol")
    rows = params // (n_epoch * n_row)
    cols = params // n_col
    width = rows + B + cols
    epochs = steps.shape[1] * n_epoch
    count = taps.shape[0]
    tile = 512
    here = steps.shape[1]
    ridge_rows = -(-rows // here)
    ridge_part = jnp.pad(ridge, (0, ridge_rows * here - rows)).reshape(ridge_rows, here)
    parts = rotated(jnp.concatenate([steps.astype(jnp.float32), ridge_part]), "epoch")
    held = rotated(jnp.stack([x[2:, : min(rows, here)].reshape(-1) for x in parts]), "prow")
    row_of = lambda x: x.reshape(1, -1)
    in_vmem = pl.BlockSpec(memory_space=pltpu.VMEM)
    f32 = lambda *shape: jax.ShapeDtypeStruct(shape, jnp.float32)
    operands = (*parts, *held, row_of(harmonic), row_of(col_scale), row_of(taps), row_of(ridge))
    vmem = lambda dtype, *shape: pltpu.VMEM(shape, dtype)
    return pl.pallas_call(
        functools.partial(main_kernel, (rows, B, cols, n_epoch, n_row)),
        grid=(epochs // (2 * tile),),
        out_shape=(f32(rows, B), f32(rows, cols)),
        in_specs=[in_vmem] * len(operands),
        out_specs=(in_vmem, in_vmem),
        scratch_shapes=[
            vmem(jnp.float32, 2 * epochs // 128, 128),
            vmem(jnp.float32, 8, epochs),
            vmem(jnp.bfloat16, 2 * count, count),
            vmem(jnp.bfloat16, B, count + 2 * tile),
            vmem(jnp.bfloat16, epochs // (2 * tile), B, 2 * tile),
            vmem(jnp.float32, B, B),
            vmem(jnp.float32, width, 128),
            vmem(jnp.float32, params, 128),
            vmem(jnp.bfloat16, width, count + tile),
            vmem(jnp.bfloat16, width, tile),
            vmem(jnp.bfloat16, width, tile),
            vmem(jnp.float32, rows + B, B + cols),
            vmem(jnp.float32, B, B),
            vmem(jnp.float32, B, 128),
        ],
        compiler_params=pltpu.CompilerParams(vmem_limit_bytes=VMEM_LIMIT),
    )(*operands)


def solution(mesh):
    in_specs = (P(None, "epoch"), P(), P(), P(), P(("epoch", "prow")))
    out_specs = (P(("epoch", "prow"), None), P(("epoch", "prow"), "pcol"))
    return jax.shard_map(
        on_device, mesh=mesh, in_specs=in_specs, out_specs=out_specs, check_vma=False
    )
```

```python
import functools
import math

import jax
import jax.numpy as jnp
from jax import lax
from jax.experimental import pallas as pl
from jax.experimental.pallas import tpu as pltpu
from jax.sharding import PartitionSpec as P

B = 256

phase_count = 4096
SINE = (6.2831640442776635, -41.337142367123384, 81.34076873476997, -70.99343163979194)
LEAD = SINE[3]
POLY = tuple(c / LEAD for c in SINE[:3])
VMEM_LIMIT = 58 * 1024 * 1024
FACTOR_BLOCK, FACTOR_GROUP, FACTOR_SLAB = 32, 4, 32


def rotated(x, axis):
    count = lax.axis_size(axis)
    shifts = [[(i, (i + k) % count) for i in range(count)] for k in range(1, count)]
    return [x] + [lax.ppermute(x, axis, pairs) for pairs in shifts]


def split3(x):
    high = x.astype(jnp.bfloat16)
    rest = x - high.astype(jnp.float32)
    mid = rest.astype(jnp.bfloat16)
    return high, mid, (rest - mid.astype(jnp.float32)).astype(jnp.bfloat16)


def dot_f32(a, b, a_dim, b_dim):
    ah, am, al = split3(a)
    bh, bm, bl = split3(b)
    return lax.dot_general(
        jnp.concatenate([ah, ah, am, ah, al, am], axis=a_dim),
        jnp.concatenate([bh, bm, bh, bl, bh, bm], axis=b_dim),
        (((a_dim,), (b_dim,)), ((), ())),
        preferred_element_type=jnp.float32,
    )


def product_f32(a, b, b_dim):
    pairs = ((0, 0), (0, 1), (1, 0), (0, 2), (2, 0), (1, 1))
    return lax.dot_general(
        jnp.concatenate([a[p] for p, _ in pairs], axis=1),
        jnp.concatenate([b[q] for _, q in pairs], axis=b_dim),
        (((1,), (b_dim,)), ((), ())),
        preferred_element_type=jnp.float32,
    )


def reciprocal(x):
    r = pl.reciprocal(x, approx=True)
    r = r * (2.0 - x * r)
    return r * (2.0 - x * r)


def factor_panel(t, size, group):
    depth = t[0].shape[0]
    row = lax.broadcasted_iota(jnp.int32, t[0].shape, 0)
    span = range(group)
    for j in range(0, size, group):
        top, at = divmod(j, depth)
        cols = [
            [jnp.broadcast_to(x[:, j + k : j + k + 1], x.shape) for x in t[top:]] for k in span
        ]
        rows = [t[top][at + k : at + k + 1, :] for k in span]
        yield
        pivot = [[cols[l][0][at + k : at + k + 1, :] for l in span] for k in span]
        done = []
        for a in range(0, group, 2):
            b = a + 1
            p, q, r = pivot[a][a], pivot[a][b], pivot[b][b]
            det = p * r - q * q
            inv = reciprocal(det)
            yield
            paa, pab, pbb = r * inv, -(q * inv), p * inv
            wa = paa * rows[a] + pab * rows[b]
            wb = pab * rows[a] + pbb * rows[b]
            for l in range(b + 1, group):
                fa = paa * pivot[a][l] + pab * pivot[b][l]
                fb = pab * pivot[a][l] + pbb * pivot[b][l]
                la, lb = pivot[l][a], pivot[l][b]
                rows[l] = rows[l] - (la * wa + lb * wb)
                cols[l] = [x - (y * fa + z * fb) for x, y, z in zip(cols[l], cols[a], cols[b])]
                for m in range(b + 1, group):
                    if m <= l:
                        ma, mb = pivot[m][a], pivot[m][b]
                        pivot[m][l] = pivot[m][l] - (ma * fa + mb * fb)
                        pivot[l][m] = pivot[m][l]
            root = lax.rsqrt(p)
            done.append(rows[a] * root)
            done.append((rows[b] - (q * root * root) * rows[a]) * lax.rsqrt(det * root * root))
            for s, (ca, cb) in enumerate(zip(cols[a], cols[b])):
                change = ca * wa + cb * wb
                if s == 0:
                    change = jnp.where(row >= at + group, change, 0.0)
                t[top + s] = t[top + s] - change
            yield
        for k in span:
            t[top] = jnp.where(row == at + k, done[k], t[top])
    return jnp.concatenate(t, axis=0) if len(t) > 1 else t[0]


def factor_step(m_ref, k, size, group, always):
    n = m_ref.shape[0]
    active = k < n // size
    here = pl.ds(pl.multiple_of(jnp.minimum(k, n // size - 1) * size, size), size)

    def ids(shape):
        return [lax.broadcasted_iota(jnp.int32, shape, d) for d in (0, 1)]

    row, lane = ids((size, 128))
    t = jnp.where(lane < size, m_ref[here, :128], jnp.where(lane - size == row, 1.0, 0.0))
    t = yield from factor_panel(
        [t[r : r + FACTOR_SLAB, :] for r in range(0, size, FACTOR_SLAB)], size, group
    )
    yield
    panel = m_ref[here, :]
    inverse = pltpu.roll(t, 128 - size, 1)[:, :size]
    head = jnp.where(lane < size, jnp.where(lane == row, 1.0, 0.0), panel[:, :128])
    yield
    done = dot_f32(inverse, jnp.concatenate([head, panel[:, 128:]], axis=1), 1, 0)
    yield
    low = dot_f32(m_ref[:, :size], inverse, 1, 1)
    yield
    low = jnp.where(ids((n, size))[0] >= (k + 1) * size, low, 0.0)
    change = dot_f32(low, done, 1, 0)
    for r in range(0, n, 32):
        yield
        full = m_ref[r : r + 32, :]
        new = jnp.where(ids((32, n))[1] < size, 0.0, full) - change[r : r + 32, :]
        new = pltpu.roll(new, n - size, 1)
        m_ref[r : r + 32, :] = new if always else jnp.where(active, new, full)
    yield
    done = pltpu.roll(done, n - size, 1)
    m_ref[here, :] = done if always else jnp.where(active, done, panel)


def fill_phases(mine, parts_refs, sums_ref, pt_ref):
    count = len(parts_refs)
    each = sums_ref.shape[0] // count
    blocks = each // 2
    for k, ref in enumerate(parts_refs):
        group = lax.rem(mine - k + count, count)
        lanes = [ref[a : a + 1, b * 128 : (b + 1) * 128] for a in range(2) for b in range(blocks)]
        rows = pl.ds(pl.multiple_of(group * each, each), each)
        sums_ref[rows, :] = jnp.concatenate(lanes, axis=0)
    total = sums_ref.shape[0]
    terms = sums_ref[...].astype(jnp.bfloat16)
    i = lax.broadcasted_iota(jnp.int32, (128, 128), 0)
    j = lax.broadcasted_iota(jnp.int32, (128, 128), 1)
    inside = jnp.dot(
        terms, jnp.where(i <= j, 1.0, 0.0).astype(jnp.bfloat16), preferred_element_type=jnp.float32
    )
    ends = jnp.dot(terms, jnp.ones((128, 128), jnp.bfloat16), preferred_element_type=jnp.float32)
    ends = ends.astype(jnp.int32)
    i = lax.broadcasted_iota(jnp.int32, (total, total), 0)
    j = lax.broadcasted_iota(jnp.int32, (total, total), 1)
    earlier = jnp.zeros((total, total), jnp.bool_)
    for track in range(2):
        mine_i = lax.rem(i, each) // blocks == track
        mine_j = lax.rem(j, each) // blocks == track
        earlier = earlier | (mine_i & mine_j & (j < i))
    earlier = jnp.where(earlier, 1.0, 0.0).astype(jnp.bfloat16)

    def before(x):
        return jnp.dot(
            earlier, x.astype(jnp.float32).astype(jnp.bfloat16), preferred_element_type=jnp.float32
        ).astype(jnp.int32)

    phase = inside.astype(jnp.int32) + before(ends & 127) + before(ends >> 7) * 128
    turn = (phase & (phase_count - 1)).astype(jnp.float32) * (1.0 / phase_count)
    pt_ref[...] = jnp.zeros_like(pt_ref)
    for r in range(total):
        group, rest = divmod(r, each)
        track, b = divmod(rest, blocks)
        lane = (group * blocks + b) * 128
        pt_ref[track : track + 1, lane : lane + 128] = turn[r : r + 1, :]


def fill_toeplitz(taps_ref, wt_ref):
    count = taps_ref.shape[1]
    taps = taps_ref[...]
    none = jnp.zeros_like(taps)
    for half, row in enumerate(([none, taps], [taps, none])):
        spread = jnp.broadcast_to(jnp.concatenate(row, axis=1), (count, 2 * count))
        spread = pltpu.roll(spread, 0, 1, stride=1, stride_axis=0)
        wt_ref[half * count : (half + 1) * count, :] = spread[:, :count].astype(jnp.bfloat16)


def parameter_table(harmonic, col_scale):
    rows = [harmonic >> 6, harmonic & 63]
    rows = [x.astype(jnp.float32) for x in rows] + [col_scale * (math.sqrt(2.0) * LEAD)]
    return jnp.concatenate(rows + [jnp.zeros((125, harmonic.shape[1]), jnp.float32)]).T


def fill_design(h_ref, pt_ref, d_ref, start, stop, lane, tile):
    here = slice(start, stop)
    p0 = pt_ref[0:1, pl.ds(tile, 256)]
    p1 = pt_ref[1:2, pl.ds(tile, 256)]
    turns = h_ref[here, 0:1] * p0 + h_ref[here, 1:2] * p1 - 0.125
    s = 0.25 - jnp.abs(turns - jnp.round(turns))
    z = s * s
    poly = ((z + POLY[2]) * z + POLY[1]) * z + POLY[0]
    d_ref[here, lane : lane + 256] = (poly * (s * h_ref[here, 2:3])).astype(jnp.bfloat16)


def fill_filtered(d_ref, wt_ref, f_ref, start, stop, block):
    count = wt_ref.shape[1]
    f_ref[start:stop, block * count : (block + 1) * count] = jnp.dot(
        d_ref[start:stop, block * count : (block + 2) * count],
        wt_ref[...],
        preferred_element_type=jnp.float32,
    ).astype(jnp.bfloat16)


def fill_lead(h_ref, pt_ref, wt_ref, d_ref, lead_ref, block_ref):
    tiles, lead, tile = lead_ref.shape
    epochs = pt_ref.shape[1]
    count = wt_ref.shape[1]
    blocks = tile // count
    d_ref[:, :count] = jnp.zeros((lead, count), jnp.bfloat16)
    block_ref[...] = jnp.zeros_like(block_ref)

    def design(start, block):
        for row in range(0, lead, 16):
            fill_design(
                h_ref, pt_ref, d_ref, row, row + 16, (block + 1) * count, start + block * count
            )

    for b in range(blocks):
        design(0, b)

    @pl.loop(0, tiles)
    def _(step):
        following = pl.multiple_of(lax.rem((step + 1) * tile, epochs), tile)
        out_ref = lead_ref.at[step]
        for b in range(blocks):
            fill_filtered(d_ref, wt_ref, out_ref, 0, lead, b)
            if b == min(1, blocks - 1):
                d_ref[:, :count] = d_ref[:, tile:]
            if b > 0:
                design(following, b - 1)
        design(following, blocks - 1)
        block_ref[...] += lax.dot_general(
            out_ref[...], out_ref[...], (((1,), (1,)), ((), ())), preferred_element_type=jnp.float32
        )


def main_kernel(shape, *refs):
    rows, lead, cols, n_epoch, n_row = shape
    parts_refs, refs = refs[:n_epoch], refs[n_epoch:]
    held_refs, refs = refs[:n_row], refs[n_row:]
    harmonic_ref, scale_ref, taps_ref, ridge_ref, panel_out, schur_out = refs[:6]
    sums_ref, pt_ref, wt_ref, dl_ref, lead_ref, block_ref = refs[6:12]
    h_ref, r_ref, d_ref, fa_ref, fb_ref, acc_ref, m_ref, first_ref = refs[12:20]
    panel_ref, schur_ref, sem = refs[20:]
    width, tile = fa_ref.shape
    count = wt_ref.shape[1]
    step = pl.program_id(0)
    epochs = pt_ref.shape[1]
    mine = lax.axis_index("epoch") * n_row + lax.axis_index("prow")
    first_row = pl.multiple_of(mine * rows, rows)
    first_col = pl.multiple_of(lax.axis_index("pcol") * cols, cols)
    segments = [(0, rows), (rows + lead, width)]
    chunks = [(at, min(at + 256, stop)) for start, stop in segments for at in range(start, stop, 256)]
    n_lead_chunks = -(-rows // 256)

    def design(start, row):
        def run():
            d_ref[row : row + 16, :count] = d_ref[row : row + 16, tile:]
            for lane in range(0, tile, 256):
                fill_design(h_ref, pt_ref, d_ref, row, row + 16, count + lane, start + lane)
        return run

    def filtered(f_ref, begin, end, block):
        return lambda: fill_filtered(d_ref, wt_ref, f_ref, begin, end, block)

    def product(f_ref, begin, end, depth):
        def run():
            acc_ref[:depth, begin:end] += lax.dot_general(
                f_ref[:depth, :],
                f_ref[rows + begin : rows + end, :],
                (((1,), (1,)), ((), ())),
                preferred_element_type=jnp.float32,
            )
        return run

    def products(f_ref):
        pieces = [(0, lead, rows)]
        pieces += [(c, min(c + 256, lead + cols), rows + lead) for c in range(lead, lead + cols, 256)]
        return [(product(f_ref, *p), (p[1] - p[0]) * p[2] * tile) for p in pieces]

    @pl.when(step == 0)
    def _():
        fill_phases(lax.axis_index("epoch"), parts_refs, sums_ref, pt_ref)
        fill_toeplitz(taps_ref, wt_ref)
        if rows % 128 or cols % 128:
            r_ref[...] = parameter_table(harmonic_ref[...], scale_ref[...])
            h_ref[:rows, :] = r_ref[pl.ds(first_row, rows), :]
            h_ref[rows + lead :, :] = r_ref[pl.ds(first_col, cols), :]
        else:
            for at, first, size in ((0, first_row, rows), (rows + lead, first_col, cols)):
                span = pl.ds(first, size)
                h_ref[at : at + size, :] = parameter_table(harmonic_ref[:, span], scale_ref[:, span])
            r_ref[:lead, :] = parameter_table(harmonic_ref[:, :lead], scale_ref[:, :lead])
        fill_lead(r_ref, pt_ref, wt_ref, dl_ref, lead_ref, block_ref)
        acc_ref[...] = jnp.zeros_like(acc_ref)
        d_ref[...] = jnp.zeros_like(d_ref)
        first = []
        for q in range(-(-lead // rows)):
            for k, ref in enumerate(held_refs):
                group = lax.rem(lax.axis_index("prow") - k + n_row, n_row)
                block = lax.rem(lax.axis_index("epoch") - q // n_row + n_epoch, n_epoch)
                term = jnp.where(group == q % n_row, ref[pl.ds(block, 1), :rows], 0.0)
                total = term if k == 0 else total + term
            first.append(total)
        first = jnp.concatenate(first, axis=1)[:, :lead]
        first_ref[...] = jnp.concatenate([first, jnp.zeros((127, lead), jnp.float32)]).T
        i = lax.broadcasted_iota(jnp.int32, (lead, lead), 0)
        j = lax.broadcasted_iota(jnp.int32, (lead, lead), 1)
        m_ref[...] = block_ref[...] * (1.0 / epochs) + jnp.where(i == j, first_ref[:, :1], 0.0)
        for begin, end in segments:
            for row in range(begin, end, 16):
                design(0, row)()

    def phase(f_ref, half, extra):
        following = pl.multiple_of(lax.rem((2 * step + half + 1) * tile, epochs), tile)
        f_ref[rows : rows + lead, :] = lead_ref[step, :, half * tile : (half + 1) * tile]
        work, ready = [], []

        def filters(begin, end):
            for b in range(tile // count):
                work.append((filtered(f_ref, begin, end, b), (end - begin) * 2 * count * count, None))
            work[-1] = (*work[-1][:2], range(begin, end, 16))

        pieces = products(f_ref)
        for begin, end in chunks[:n_lead_chunks]:
            filters(begin, end)
        for n, (begin, end) in enumerate(chunks[n_lead_chunks:]):
            filters(begin, end)
            work.append((*pieces[n], None))
        for piece in pieces[len(chunks) - n_lead_chunks :]:
            work.append((*piece, None))
        total, spent, given = sum(w[1] for w in work), 0, 0
        every = sum(end - begin for begin, end in chunks) // 16
        for run, cost, rows_done in work:
            run()
            spent += cost
            ready += list(rows_done or ())
            while given < every * spent // total and ready:
                design(following, ready.pop(0))()
                next(extra, None)
                given += 1
        for row in ready:
            design(following, row)()
            next(extra, None)

    always = epochs // (2 * tile) <= lead // FACTOR_BLOCK
    factor = factor_step(m_ref, step, FACTOR_BLOCK, FACTOR_GROUP, always)
    phase(fa_ref, 0, factor)
    phase(fb_ref, 1, factor)
    for _ in factor:
        pass

    @pl.when(step == pl.num_programs(0) - 1)
    def _():
        mid = -(-rows // 128) * 128
        own = ridge_ref[...]
        if mid > rows:
            own = jnp.concatenate([own, jnp.zeros((1, mid - rows), jnp.float32)], axis=1)
        own = jnp.concatenate([own, jnp.zeros((127, mid), jnp.float32)]).T[:rows, :1]
        first = first_ref[:, :1]
        scale = 1.0 / epochs
        @pl.loop(epochs // (2 * tile), max(lead // FACTOR_BLOCK, epochs // (2 * tile)))
        def _(k):
            for _ in factor_step(m_ref, k, FACTOR_BLOCK, FACTOR_GROUP, True):
                pass

        def total(begin, end, first, width_of, first_id, diagonal):
            i = lax.broadcasted_iota(jnp.int32, (end - begin, width_of), 0)
            j = lax.broadcasted_iota(jnp.int32, (end - begin, width_of), 1) + first_id
            i = i + first_row if begin == 0 else i
            block = acc_ref[begin:end, first : first + width_of]
            return block * scale + jnp.where(i == j, diagonal, 0.0)

        i = lax.broadcasted_iota(jnp.int32, (lead, lead), 0)
        j = lax.broadcasted_iota(jnp.int32, (lead, lead), 1)
        inverse = split3(jnp.where(i >= j, m_ref[...], 0.0))
        panel = product_f32(split3(total(0, rows, 0, lead, 0, own)), inverse, 1)
        panel_ref[...] = panel
        copies = [pltpu.make_async_copy(panel_ref, panel_out, sem.at[0])]
        copies[0].start()
        panel = split3(panel)
        for n, c in enumerate(range(0, cols, 256)):
            size = min(256, cols - c)
            span = slice(c, c + size)
            right = total(rows, rows + lead, lead + c, size, first_col + c, first)
            solved = split3(product_f32(inverse, split3(right), 0))
            left = total(0, rows, lead + c, size, first_col + c, own)
            schur_ref[:, span] = left - product_f32(panel, solved, 0)
            copies.append(
                pltpu.make_async_copy(schur_ref.at[:, span], schur_out.at[:, span], sem.at[n + 1])
            )
            copies[-1].start()
        for copy in copies:
            copy.wait()


def on_device(steps, harmonic, col_scale, taps, ridge):
    params = harmonic.shape[0]
    n_epoch = lax.axis_size("epoch")
    n_row = lax.axis_size("prow")
    n_col = lax.axis_size("pcol")
    rows = params // (n_epoch * n_row)
    cols = params // n_col
    width = rows + B + cols
    epochs = steps.shape[1] * n_epoch
    count = taps.shape[0]
    tile = 512
    here = steps.shape[1]
    ridge_rows = -(-rows // here)
    ridge_part = jnp.pad(ridge, (0, ridge_rows * here - rows)).reshape(ridge_rows, here)
    packed = jnp.pad(steps, ((0, ridge_rows), (0, 0))).astype(jnp.float32)
    parts = rotated(packed + jnp.pad(ridge_part, ((2, 0), (0, 0))), "epoch")
    held = rotated(jnp.stack([x[2:, : min(rows, here)].reshape(-1) for x in parts]), "prow")
    row_of = lambda x: x.reshape(1, -1)
    in_vmem = pl.BlockSpec(memory_space=pltpu.VMEM)
    f32 = lambda *shape: jax.ShapeDtypeStruct(shape, jnp.float32)
    operands = (*parts, *held, row_of(harmonic), row_of(col_scale), row_of(taps), row_of(ridge))
    vmem = lambda dtype, *shape: pltpu.VMEM(shape, dtype)
    return pl.pallas_call(
        functools.partial(main_kernel, (rows, B, cols, n_epoch, n_row)),
        grid=(epochs // (2 * tile),),
        out_shape=(f32(rows, B), f32(rows, cols)),
        in_specs=[in_vmem] * len(operands),
        out_specs=(pl.BlockSpec(memory_space=pl.ANY),) * 2,
        scratch_shapes=[
            vmem(jnp.float32, 2 * epochs // 128, 128),
            vmem(jnp.float32, 8, epochs),
            vmem(jnp.bfloat16, 2 * count, count),
            vmem(jnp.bfloat16, B, count + 2 * tile),
            vmem(jnp.bfloat16, epochs // (2 * tile), B, 2 * tile),
            vmem(jnp.float32, B, B),
            vmem(jnp.float32, width, 128),
            vmem(jnp.float32, params, 128),
            vmem(jnp.bfloat16, width, count + tile),
            vmem(jnp.bfloat16, width, tile),
            vmem(jnp.bfloat16, width, tile),
            vmem(jnp.float32, rows + B, B + cols),
            vmem(jnp.float32, B, B),
            vmem(jnp.float32, B, 128),
            vmem(jnp.float32, rows, B),
            vmem(jnp.float32, rows, cols),
            pltpu.SemaphoreType.DMA((1 + -(-cols // 256),)),
        ],
        compiler_params=pltpu.CompilerParams(vmem_limit_bytes=VMEM_LIMIT),
    )(*operands)


def solution(mesh):
    in_specs = (P(None, "epoch"), P(), P(), P(), P(("epoch", "prow")))
    out_specs = (P(("epoch", "prow"), None), P(("epoch", "prow"), "pcol"))
    return jax.shard_map(
        on_device, mesh=mesh, in_specs=in_specs, out_specs=out_specs, check_vma=False
    )
```

```python
import functools
import math

import jax
import jax.numpy as jnp
from jax import lax
from jax.experimental import pallas as pl
from jax.experimental.pallas import tpu as pltpu
from jax.sharding import PartitionSpec as P

B = 256

phase_count = 4096
SINE = (6.2831640442776635, -41.337142367123384, 81.34076873476997, -70.99343163979194)
LEAD = SINE[3]
POLY = tuple(c / LEAD for c in SINE[:3])
VMEM_LIMIT = 58 * 1024 * 1024
FACTOR_BLOCK, FACTOR_GROUP, FACTOR_SLAB = 32, 4, 32


def rotated(x, axis):
    count = lax.axis_size(axis)
    shifts = [[(i, (i + k) % count) for i in range(count)] for k in range(1, count)]
    return [x] + [lax.ppermute(x, axis, pairs) for pairs in shifts]


def split3(x):
    high = x.astype(jnp.bfloat16)
    rest = x - high.astype(jnp.float32)
    mid = rest.astype(jnp.bfloat16)
    return high, mid, (rest - mid.astype(jnp.float32)).astype(jnp.bfloat16)


def dot_f32(a, b, a_dim, b_dim):
    ah, am, al = split3(a)
    bh, bm, bl = split3(b)
    return lax.dot_general(
        jnp.concatenate([ah, ah, am, ah, al, am], axis=a_dim),
        jnp.concatenate([bh, bm, bh, bl, bh, bm], axis=b_dim),
        (((a_dim,), (b_dim,)), ((), ())),
        preferred_element_type=jnp.float32,
    )


def product_f32(a, b, b_dim):
    pairs = ((0, 0), (0, 1), (1, 0), (0, 2), (2, 0), (1, 1))
    return lax.dot_general(
        jnp.concatenate([a[p] for p, _ in pairs], axis=1),
        jnp.concatenate([b[q] for _, q in pairs], axis=b_dim),
        (((1,), (b_dim,)), ((), ())),
        preferred_element_type=jnp.float32,
    )


def reciprocal(x):
    r = pl.reciprocal(x, approx=True)
    r = r * (2.0 - x * r)
    return r * (2.0 - x * r)


def factor_panel(t, size, group):
    depth = t[0].shape[0]
    row = lax.broadcasted_iota(jnp.int32, t[0].shape, 0)
    span = range(group)
    for j in range(0, size, group):
        top, at = divmod(j, depth)
        cols = [
            [jnp.broadcast_to(x[:, j + k : j + k + 1], x.shape) for x in t[top:]] for k in span
        ]
        rows = [t[top][at + k : at + k + 1, :] for k in span]
        yield
        pivot = [[cols[l][0][at + k : at + k + 1, :] for l in span] for k in span]
        done = []
        for a in range(0, group, 2):
            b = a + 1
            p, q, r = pivot[a][a], pivot[a][b], pivot[b][b]
            det = p * r - q * q
            inv = reciprocal(det)
            yield
            paa, pab, pbb = r * inv, -(q * inv), p * inv
            wa = paa * rows[a] + pab * rows[b]
            wb = pab * rows[a] + pbb * rows[b]
            for l in range(b + 1, group):
                fa = paa * pivot[a][l] + pab * pivot[b][l]
                fb = pab * pivot[a][l] + pbb * pivot[b][l]
                la, lb = pivot[l][a], pivot[l][b]
                rows[l] = rows[l] - (la * wa + lb * wb)
                cols[l] = [x - (y * fa + z * fb) for x, y, z in zip(cols[l], cols[a], cols[b])]
                for m in range(b + 1, group):
                    if m <= l:
                        ma, mb = pivot[m][a], pivot[m][b]
                        pivot[m][l] = pivot[m][l] - (ma * fa + mb * fb)
                        pivot[l][m] = pivot[m][l]
            root = lax.rsqrt(p)
            done.append(rows[a] * root)
            done.append((rows[b] - (q * root * root) * rows[a]) * lax.rsqrt(det * root * root))
            for s, (ca, cb) in enumerate(zip(cols[a], cols[b])):
                change = ca * wa + cb * wb
                if s == 0:
                    change = jnp.where(row >= at + group, change, 0.0)
                t[top + s] = t[top + s] - change
            yield
        for k in span:
            t[top] = jnp.where(row == at + k, done[k], t[top])
    return jnp.concatenate(t, axis=0) if len(t) > 1 else t[0]


def factor_step(m_ref, k, size, group, always):
    n = m_ref.shape[0]
    active = k < n // size
    here = pl.ds(pl.multiple_of(jnp.minimum(k, n // size - 1) * size, size), size)

    def ids(shape):
        return [lax.broadcasted_iota(jnp.int32, shape, d) for d in (0, 1)]

    row, lane = ids((size, 128))
    t = jnp.where(lane < size, m_ref[here, :128], jnp.where(lane - size == row, 1.0, 0.0))
    t = yield from factor_panel(
        [t[r : r + FACTOR_SLAB, :] for r in range(0, size, FACTOR_SLAB)], size, group
    )
    yield
    panel = m_ref[here, :]
    inverse = pltpu.roll(t, 128 - size, 1)[:, :size]
    head = jnp.where(lane < size, jnp.where(lane == row, 1.0, 0.0), panel[:, :128])
    yield
    done = dot_f32(inverse, jnp.concatenate([head, panel[:, 128:]], axis=1), 1, 0)
    yield
    low = dot_f32(m_ref[:, :size], inverse, 1, 1)
    yield
    low = jnp.where(ids((n, size))[0] >= (k + 1) * size, low, 0.0)
    change = dot_f32(low, done, 1, 0)
    for r in range(0, n, 32):
        yield
        full = m_ref[r : r + 32, :]
        new = jnp.where(ids((32, n))[1] < size, 0.0, full) - change[r : r + 32, :]
        new = pltpu.roll(new, n - size, 1)
        m_ref[r : r + 32, :] = new if always else jnp.where(active, new, full)
    yield
    done = pltpu.roll(done, n - size, 1)
    m_ref[here, :] = done if always else jnp.where(active, done, panel)


def fill_phases(mine, parts_refs, sums_ref, pt_ref):
    count = len(parts_refs)
    each = sums_ref.shape[0] // count
    blocks = each // 2
    for k, ref in enumerate(parts_refs):
        group = lax.rem(mine - k + count, count)
        lanes = [ref[a : a + 1, b * 128 : (b + 1) * 128] for a in range(2) for b in range(blocks)]
        rows = pl.ds(pl.multiple_of(group * each, each), each)
        sums_ref[rows, :] = jnp.concatenate(lanes, axis=0)
    total = sums_ref.shape[0]
    terms = sums_ref[...].astype(jnp.bfloat16)
    i = lax.broadcasted_iota(jnp.int32, (128, 128), 0)
    j = lax.broadcasted_iota(jnp.int32, (128, 128), 1)
    inside = jnp.dot(
        terms, jnp.where(i <= j, 1.0, 0.0).astype(jnp.bfloat16), preferred_element_type=jnp.float32
    )
    ends = jnp.dot(terms, jnp.ones((128, 128), jnp.bfloat16), preferred_element_type=jnp.float32)
    ends = ends.astype(jnp.int32)
    i = lax.broadcasted_iota(jnp.int32, (total, total), 0)
    j = lax.broadcasted_iota(jnp.int32, (total, total), 1)
    earlier = jnp.zeros((total, total), jnp.bool_)
    for track in range(2):
        mine_i = lax.rem(i, each) // blocks == track
        mine_j = lax.rem(j, each) // blocks == track
        earlier = earlier | (mine_i & mine_j & (j < i))
    earlier = jnp.where(earlier, 1.0, 0.0).astype(jnp.bfloat16)

    def before(x):
        return jnp.dot(
            earlier, x.astype(jnp.float32).astype(jnp.bfloat16), preferred_element_type=jnp.float32
        ).astype(jnp.int32)

    phase = inside.astype(jnp.int32) + before(ends & 127) + before(ends >> 7) * 128
    turn = (phase & (phase_count - 1)).astype(jnp.float32) * (1.0 / phase_count)
    pt_ref[...] = jnp.zeros_like(pt_ref)
    for r in range(total):
        group, rest = divmod(r, each)
        track, b = divmod(rest, blocks)
        lane = (group * blocks + b) * 128
        pt_ref[track : track + 1, lane : lane + 128] = turn[r : r + 1, :]


def fill_toeplitz(taps_ref, wt_ref):
    count = taps_ref.shape[1]
    taps = taps_ref[...]
    none = jnp.zeros_like(taps)
    for half, row in enumerate(([none, taps], [taps, none])):
        spread = jnp.broadcast_to(jnp.concatenate(row, axis=1), (count, 2 * count))
        spread = pltpu.roll(spread, 0, 1, stride=1, stride_axis=0)
        wt_ref[half * count : (half + 1) * count, :] = spread[:, :count].astype(jnp.bfloat16)


def parameter_table(harmonic, col_scale):
    rows = [harmonic >> 6, harmonic & 63]
    rows = [x.astype(jnp.float32) for x in rows] + [col_scale * (math.sqrt(2.0) * LEAD)]
    return jnp.concatenate(rows + [jnp.zeros((125, harmonic.shape[1]), jnp.float32)]).T


def fill_design(h_ref, pt_ref, d_ref, start, stop, lane, tile):
    here = slice(start, stop)
    p0 = pt_ref[0:1, pl.ds(tile, 256)]
    p1 = pt_ref[1:2, pl.ds(tile, 256)]
    turns = h_ref[here, 0:1] * p0 + h_ref[here, 1:2] * p1 - 0.125
    s = 0.25 - jnp.abs(turns - jnp.round(turns))
    z = s * s
    poly = ((z + POLY[2]) * z + POLY[1]) * z + POLY[0]
    d_ref[here, lane : lane + 256] = (poly * (s * h_ref[here, 2:3])).astype(jnp.bfloat16)


def fill_filtered(d_ref, wt_ref, f_ref, start, stop, block):
    count = wt_ref.shape[1]
    f_ref[start:stop, block * count : (block + 1) * count] = jnp.dot(
        d_ref[start:stop, block * count : (block + 2) * count],
        wt_ref[...],
        preferred_element_type=jnp.float32,
    ).astype(jnp.bfloat16)


def fill_lead(h_ref, pt_ref, wt_ref, d_ref, lead_ref, block_ref):
    tiles, lead, tile = lead_ref.shape
    epochs = pt_ref.shape[1]
    count = wt_ref.shape[1]
    blocks = tile // count
    d_ref[:, :count] = jnp.zeros((lead, count), jnp.bfloat16)
    block_ref[...] = jnp.zeros_like(block_ref)

    def design(start, block):
        for row in range(0, lead, 16):
            fill_design(
                h_ref, pt_ref, d_ref, row, row + 16, (block + 1) * count, start + block * count
            )

    for b in range(blocks):
        design(0, b)

    @pl.loop(0, tiles, unroll=2 - tiles % 2)
    def _(step):
        following = pl.multiple_of(lax.rem((step + 1) * tile, epochs), tile)
        out_ref = lead_ref.at[step]
        for b in range(blocks):
            fill_filtered(d_ref, wt_ref, out_ref, 0, lead, b)
            if b == min(1, blocks - 1):
                d_ref[:, :count] = d_ref[:, tile:]
            if b > 0:
                design(following, b - 1)
        design(following, blocks - 1)
        block_ref[...] += lax.dot_general(
            out_ref[...], out_ref[...], (((1,), (1,)), ((), ())), preferred_element_type=jnp.float32
        )


def main_kernel(shape, *refs):
    rows, lead, cols, n_epoch, n_row = shape
    parts_refs, refs = refs[:n_epoch], refs[n_epoch:]
    harmonic_ref, scale_ref, taps_ref, ridge_ref, panel_out, schur_out = refs[:6]
    sums_ref, pt_ref, wt_ref, dl_ref, lead_ref, block_ref = refs[6:12]
    h_ref, r_ref, d_ref, fa_ref, fb_ref, acc_ref, m_ref, first_ref = refs[12:20]
    panel_ref, schur_ref, sem = refs[20:]
    width, tile = fa_ref.shape
    count = wt_ref.shape[1]
    step = pl.program_id(0)
    epochs = pt_ref.shape[1]
    mine = lax.axis_index("epoch") * n_row + lax.axis_index("prow")
    first_row = pl.multiple_of(mine * rows, rows)
    first_col = pl.multiple_of(lax.axis_index("pcol") * cols, cols)
    segments = [(0, rows), (rows + lead, width)]
    chunks = [(at, min(at + 256, stop)) for start, stop in segments for at in range(start, stop, 256)]
    n_lead_chunks = -(-rows // 256)

    def design(start, row):
        def run():
            d_ref[row : row + 16, :count] = d_ref[row : row + 16, tile:]
            for lane in range(0, tile, 256):
                fill_design(h_ref, pt_ref, d_ref, row, row + 16, count + lane, start + lane)
        return run

    def filtered(f_ref, begin, end, block):
        return lambda: fill_filtered(d_ref, wt_ref, f_ref, begin, end, block)

    def product(f_ref, begin, end, depth):
        def run():
            acc_ref[:depth, begin:end] += lax.dot_general(
                f_ref[:depth, :],
                f_ref[rows + begin : rows + end, :],
                (((1,), (1,)), ((), ())),
                preferred_element_type=jnp.float32,
            )
        return run

    def products(f_ref):
        pieces = [(0, lead, rows)]
        pieces += [(c, min(c + 256, lead + cols), rows + lead) for c in range(lead, lead + cols, 256)]
        return [(product(f_ref, *p), (p[1] - p[0]) * p[2] * tile) for p in pieces]

    @pl.when(step == 0)
    def _():
        fill_phases(lax.axis_index("epoch"), parts_refs, sums_ref, pt_ref)
        fill_toeplitz(taps_ref, wt_ref)
        if rows % 128 or cols % 128:
            r_ref[...] = parameter_table(harmonic_ref[...], scale_ref[...])
            h_ref[:rows, :] = r_ref[pl.ds(first_row, rows), :]
            h_ref[rows + lead :, :] = r_ref[pl.ds(first_col, cols), :]
        else:
            for at, first, size in ((0, first_row, rows), (rows + lead, first_col, cols)):
                span = pl.ds(first, size)
                h_ref[at : at + size, :] = parameter_table(harmonic_ref[:, span], scale_ref[:, span])
            r_ref[:lead, :] = parameter_table(harmonic_ref[:, :lead], scale_ref[:, :lead])
        fill_lead(r_ref, pt_ref, wt_ref, dl_ref, lead_ref, block_ref)
        acc_ref[...] = jnp.zeros_like(acc_ref)
        d_ref[...] = jnp.zeros_like(d_ref)
        first = []
        local = parts_refs[0].shape[1]
        deep = -(-rows // local)
        for q in range(-(-lead // rows)):
            total = jnp.zeros((1, rows), jnp.float32)
            for e, ref in enumerate(parts_refs):
                for k in range(n_row):
                    group = lax.rem(lax.axis_index("epoch") - e + n_epoch, n_epoch)
                    row_group = lax.rem(lax.axis_index("prow") - k + n_row, n_row)
                    held = [ref[2 + k * deep + d : 3 + k * deep + d, :] for d in range(deep)]
                    held = jnp.concatenate(held, axis=1)[:, :rows]
                    found = (group == q // n_row) & (row_group == q % n_row)
                    total = total + jnp.where(found, held, 0.0)
            first.append(total)
        first = jnp.concatenate(first, axis=1)[:, :lead]
        first_ref[...] = jnp.concatenate([first, jnp.zeros((127, lead), jnp.float32)]).T
        i = lax.broadcasted_iota(jnp.int32, (lead, lead), 0)
        j = lax.broadcasted_iota(jnp.int32, (lead, lead), 1)
        m_ref[...] = block_ref[...] * (1.0 / epochs) + jnp.where(i == j, first_ref[:, :1], 0.0)
        for begin, end in segments:
            for row in range(begin, end, 16):
                design(0, row)()

    def phase(f_ref, half, extra):
        following = pl.multiple_of(lax.rem((2 * step + half + 1) * tile, epochs), tile)
        f_ref[rows : rows + lead, :] = lead_ref[step, :, half * tile : (half + 1) * tile]
        work, ready = [], []

        def filters(begin, end):
            for b in range(tile // count):
                work.append((filtered(f_ref, begin, end, b), (end - begin) * 2 * count * count, None))
            work[-1] = (*work[-1][:2], range(begin, end, 16))

        pieces = products(f_ref)
        for begin, end in chunks[:n_lead_chunks]:
            filters(begin, end)
        for n, (begin, end) in enumerate(chunks[n_lead_chunks:]):
            filters(begin, end)
            work.append((*pieces[n], None))
        for piece in pieces[len(chunks) - n_lead_chunks :]:
            work.append((*piece, None))
        total, spent, given = sum(w[1] for w in work), 0, 0
        every = sum(end - begin for begin, end in chunks) // 16
        for run, cost, rows_done in work:
            run()
            spent += cost
            ready += list(rows_done or ())
            while given < every * spent // total and ready:
                design(following, ready.pop(0))()
                next(extra, None)
                given += 1
        for row in ready:
            design(following, row)()
            next(extra, None)

    always = epochs // (2 * tile) <= lead // FACTOR_BLOCK
    factor = factor_step(m_ref, step, FACTOR_BLOCK, FACTOR_GROUP, always)
    phase(fa_ref, 0, factor)
    phase(fb_ref, 1, factor)
    for _ in factor:
        pass

    @pl.when(step == pl.num_programs(0) - 1)
    def _():
        mid = -(-rows // 128) * 128
        own = ridge_ref[...]
        if mid > rows:
            own = jnp.concatenate([own, jnp.zeros((1, mid - rows), jnp.float32)], axis=1)
        own = jnp.concatenate([own, jnp.zeros((127, mid), jnp.float32)]).T[:rows, :1]
        first = first_ref[:, :1]
        scale = 1.0 / epochs
        @pl.loop(epochs // (2 * tile), max(lead // FACTOR_BLOCK, epochs // (2 * tile)))
        def _(k):
            for _ in factor_step(m_ref, k, FACTOR_BLOCK, FACTOR_GROUP, True):
                pass

        def total(begin, end, first, width_of, first_id, diagonal):
            i = lax.broadcasted_iota(jnp.int32, (end - begin, width_of), 0)
            j = lax.broadcasted_iota(jnp.int32, (end - begin, width_of), 1) + first_id
            i = i + first_row if begin == 0 else i
            block = acc_ref[begin:end, first : first + width_of]
            return block * scale + jnp.where(i == j, diagonal, 0.0)

        i = lax.broadcasted_iota(jnp.int32, (lead, lead), 0)
        j = lax.broadcasted_iota(jnp.int32, (lead, lead), 1)
        inverse = split3(jnp.where(i >= j, m_ref[...], 0.0))
        panel = product_f32(split3(total(0, rows, 0, lead, 0, own)), inverse, 1)
        panel_ref[...] = panel
        copies = [pltpu.make_async_copy(panel_ref, panel_out, sem.at[0])]
        copies[0].start()
        panel = split3(panel)
        for n, c in enumerate(range(0, cols, 256)):
            size = min(256, cols - c)
            span = slice(c, c + size)
            right = total(rows, rows + lead, lead + c, size, first_col + c, first)
            solved = split3(product_f32(inverse, split3(right), 0))
            left = total(0, rows, lead + c, size, first_col + c, own)
            schur_ref[:, span] = left - product_f32(panel, solved, 0)
            copies.append(
                pltpu.make_async_copy(schur_ref.at[:, span], schur_out.at[:, span], sem.at[n + 1])
            )
            copies[-1].start()
        for copy in copies:
            copy.wait()


def on_device(steps, harmonic, col_scale, taps, ridge):
    params = harmonic.shape[0]
    n_epoch = lax.axis_size("epoch")
    n_row = lax.axis_size("prow")
    n_col = lax.axis_size("pcol")
    rows = params // (n_epoch * n_row)
    cols = params // n_col
    width = rows + B + cols
    epochs = steps.shape[1] * n_epoch
    count = taps.shape[0]
    tile = 512
    here = steps.shape[1]
    ridge_rows = -(-rows // here)
    packed = jnp.pad(steps, ((0, n_row * ridge_rows), (0, 0))).astype(jnp.float32)
    for k, x in enumerate(rotated(ridge, "prow")):
        x = jnp.pad(x, (0, ridge_rows * here - rows)).reshape(ridge_rows, here)
        packed = packed + jnp.pad(x, ((2 + k * ridge_rows, (n_row - 1 - k) * ridge_rows), (0, 0)))
    parts = rotated(packed, "epoch")
    row_of = lambda x: x.reshape(1, -1)
    in_vmem = pl.BlockSpec(memory_space=pltpu.VMEM)
    f32 = lambda *shape: jax.ShapeDtypeStruct(shape, jnp.float32)
    operands = (*parts, row_of(harmonic), row_of(col_scale), row_of(taps), row_of(ridge))
    vmem = lambda dtype, *shape: pltpu.VMEM(shape, dtype)
    return pl.pallas_call(
        functools.partial(main_kernel, (rows, B, cols, n_epoch, n_row)),
        grid=(epochs // (2 * tile),),
        out_shape=(f32(rows, B), f32(rows, cols)),
        in_specs=[in_vmem] * len(operands),
        out_specs=(pl.BlockSpec(memory_space=pl.ANY),) * 2,
        scratch_shapes=[
            vmem(jnp.float32, 2 * epochs // 128, 128),
            vmem(jnp.float32, 8, epochs),
            vmem(jnp.bfloat16, 2 * count, count),
            vmem(jnp.bfloat16, B, count + 2 * tile),
            vmem(jnp.bfloat16, epochs // (2 * tile), B, 2 * tile),
            vmem(jnp.float32, B, B),
            vmem(jnp.float32, width, 128),
            vmem(jnp.float32, params, 128),
            vmem(jnp.bfloat16, width, count + tile),
            vmem(jnp.bfloat16, width, tile),
            vmem(jnp.bfloat16, width, tile),
            vmem(jnp.float32, rows + B, B + cols),
            vmem(jnp.float32, B, B),
            vmem(jnp.float32, B, 128),
            vmem(jnp.float32, rows, B),
            vmem(jnp.float32, rows, cols),
            pltpu.SemaphoreType.DMA((1 + -(-cols // 256),)),
        ],
        compiler_params=pltpu.CompilerParams(vmem_limit_bytes=VMEM_LIMIT),
    )(*operands)


def solution(mesh):
    in_specs = (P(None, "epoch"), P(), P(), P(), P(("epoch", "prow")))
    out_specs = (P(("epoch", "prow"), None), P(("epoch", "prow"), "pcol"))
    return jax.shard_map(
        on_device, mesh=mesh, in_specs=in_specs, out_specs=out_specs, check_vma=False
    )
```

```python
import functools
import math

import jax
import jax.numpy as jnp
from jax import lax
from jax.experimental import pallas as pl
from jax.experimental.pallas import tpu as pltpu
from jax.sharding import PartitionSpec as P

B = 256

phase_count = 4096
SINE = (6.2831640442776635, -41.337142367123384, 81.34076873476997, -70.99343163979194)
LEAD = SINE[3]
POLY = tuple(c / LEAD for c in SINE[:3])
VMEM_LIMIT = 58 * 1024 * 1024
FACTOR_BLOCK, FACTOR_GROUP, FACTOR_SLAB = 32, 8, 8


def rotated(x, axis):
    count = lax.axis_size(axis)
    shifts = [[(i, (i + k) % count) for i in range(count)] for k in range(1, count)]
    return [x] + [lax.ppermute(x, axis, pairs) for pairs in shifts]


def split3(x):
    high = x.astype(jnp.bfloat16)
    rest = x - high.astype(jnp.float32)
    mid = rest.astype(jnp.bfloat16)
    return high, mid, (rest - mid.astype(jnp.float32)).astype(jnp.bfloat16)


def dot_f32(a, b, a_dim, b_dim):
    ah, am, al = split3(a)
    bh, bm, bl = split3(b)
    return lax.dot_general(
        jnp.concatenate([ah, ah, am, ah, al, am], axis=a_dim),
        jnp.concatenate([bh, bm, bh, bl, bh, bm], axis=b_dim),
        (((a_dim,), (b_dim,)), ((), ())),
        preferred_element_type=jnp.float32,
    )


def product_f32(a, b, b_dim):
    pairs = ((0, 0), (0, 1), (1, 0), (0, 2), (2, 0), (1, 1))
    return lax.dot_general(
        jnp.concatenate([a[p] for p, _ in pairs], axis=1),
        jnp.concatenate([b[q] for _, q in pairs], axis=b_dim),
        (((1,), (b_dim,)), ((), ())),
        preferred_element_type=jnp.float32,
    )


def reciprocal(x):
    r = pl.reciprocal(x, approx=True)
    r = r * (2.0 - x * r)
    return r * (2.0 - x * r)


def factor_panel(t, size, group):
    depth = t[0].shape[0]
    row = lax.broadcasted_iota(jnp.int32, t[0].shape, 0)
    span = range(group)
    for j in range(0, size, group):
        top, at = divmod(j, depth)
        cols = [
            [jnp.broadcast_to(x[:, j + k : j + k + 1], x.shape) for x in t[top:]] for k in span
        ]
        rows = [t[top][at + k : at + k + 1, :] for k in span]
        yield
        pivot = [[cols[l][0][at + k : at + k + 1, :] for l in span] for k in span]
        done = []
        for a in range(0, group, 2):
            b = a + 1
            p, q, r = pivot[a][a], pivot[a][b], pivot[b][b]
            det = p * r - q * q
            inv = reciprocal(det)
            yield
            paa, pab, pbb = r * inv, -(q * inv), p * inv
            wa = paa * rows[a] + pab * rows[b]
            wb = pab * rows[a] + pbb * rows[b]
            for l in range(b + 1, group):
                fa = paa * pivot[a][l] + pab * pivot[b][l]
                fb = pab * pivot[a][l] + pbb * pivot[b][l]
                la, lb = pivot[l][a], pivot[l][b]
                rows[l] = rows[l] - (la * wa + lb * wb)
                cols[l] = [x - (y * fa + z * fb) for x, y, z in zip(cols[l], cols[a], cols[b])]
                for m in range(b + 1, group):
                    if m <= l:
                        ma, mb = pivot[m][a], pivot[m][b]
                        pivot[m][l] = pivot[m][l] - (ma * fa + mb * fb)
                        pivot[l][m] = pivot[m][l]
            root = lax.rsqrt(p)
            done.append(rows[a] * root)
            done.append((rows[b] - (q * root * root) * rows[a]) * lax.rsqrt(det * root * root))
            for s, (ca, cb) in enumerate(zip(cols[a], cols[b])):
                change = ca * wa + cb * wb
                if s == 0:
                    change = jnp.where(row >= at + group, change, 0.0)
                t[top + s] = t[top + s] - change
            yield
        for k in span:
            t[top] = jnp.where(row == at + k, done[k], t[top])
    return jnp.concatenate(t, axis=0) if len(t) > 1 else t[0]


def factor_step(m_ref, k, size, group, always):
    n = m_ref.shape[0]
    active = k < n // size
    here = pl.ds(pl.multiple_of(jnp.minimum(k, n // size - 1) * size, size), size)

    def ids(shape):
        return [lax.broadcasted_iota(jnp.int32, shape, d) for d in (0, 1)]

    row, lane = ids((size, 128))
    t = jnp.where(lane < size, m_ref[here, :128], jnp.where(lane - size == row, 1.0, 0.0))
    t = yield from factor_panel(
        [t[r : r + FACTOR_SLAB, :] for r in range(0, size, FACTOR_SLAB)], size, group
    )
    yield
    panel = m_ref[here, :]
    inverse = pltpu.roll(t, 128 - size, 1)[:, :size]
    head = jnp.where(lane < size, jnp.where(lane == row, 1.0, 0.0), panel[:, :128])
    yield
    done = dot_f32(inverse, jnp.concatenate([head, panel[:, 128:]], axis=1), 1, 0)
    yield
    low = dot_f32(m_ref[:, :size], inverse, 1, 1)
    yield
    low = jnp.where(ids((n, size))[0] >= (k + 1) * size, low, 0.0)
    change = dot_f32(low, done, 1, 0)
    for r in range(0, n, 32):
        yield
        full = m_ref[r : r + 32, :]
        new = jnp.where(ids((32, n))[1] < size, 0.0, full) - change[r : r + 32, :]
        new = pltpu.roll(new, n - size, 1)
        m_ref[r : r + 32, :] = new if always else jnp.where(active, new, full)
    yield
    done = pltpu.roll(done, n - size, 1)
    m_ref[here, :] = done if always else jnp.where(active, done, panel)


def fill_phases(mine, parts_refs, sums_ref, pt_ref):
    count = len(parts_refs)
    each = sums_ref.shape[0] // count
    blocks = each // 2
    for k, ref in enumerate(parts_refs):
        group = lax.rem(mine - k + count, count)
        lanes = [ref[a : a + 1, b * 128 : (b + 1) * 128] for a in range(2) for b in range(blocks)]
        rows = pl.ds(pl.multiple_of(group * each, each), each)
        sums_ref[rows, :] = jnp.concatenate(lanes, axis=0)
    total = sums_ref.shape[0]
    terms = sums_ref[...].astype(jnp.bfloat16)
    i = lax.broadcasted_iota(jnp.int32, (128, 128), 0)
    j = lax.broadcasted_iota(jnp.int32, (128, 128), 1)
    inside = jnp.dot(
        terms, jnp.where(i <= j, 1.0, 0.0).astype(jnp.bfloat16), preferred_element_type=jnp.float32
    )
    ends = jnp.dot(terms, jnp.ones((128, 128), jnp.bfloat16), preferred_element_type=jnp.float32)
    ends = ends.astype(jnp.int32)
    i = lax.broadcasted_iota(jnp.int32, (total, total), 0)
    j = lax.broadcasted_iota(jnp.int32, (total, total), 1)
    earlier = jnp.zeros((total, total), jnp.bool_)
    for track in range(2):
        mine_i = lax.rem(i, each) // blocks == track
        mine_j = lax.rem(j, each) // blocks == track
        earlier = earlier | (mine_i & mine_j & (j < i))
    earlier = jnp.where(earlier, 1.0, 0.0).astype(jnp.bfloat16)

    def before(x):
        return jnp.dot(
            earlier, x.astype(jnp.float32).astype(jnp.bfloat16), preferred_element_type=jnp.float32
        ).astype(jnp.int32)

    phase = inside.astype(jnp.int32) + before(ends & 127) + before(ends >> 7) * 128
    turn = (phase & (phase_count - 1)).astype(jnp.float32) * (1.0 / phase_count)
    pt_ref[...] = jnp.zeros_like(pt_ref)
    for r in range(total):
        group, rest = divmod(r, each)
        track, b = divmod(rest, blocks)
        lane = (group * blocks + b) * 128
        pt_ref[track : track + 1, lane : lane + 128] = turn[r : r + 1, :]


def fill_toeplitz(taps_ref, wt_ref):
    count = taps_ref.shape[1]
    taps = taps_ref[...]
    none = jnp.zeros_like(taps)
    for half, row in enumerate(([none, taps], [taps, none])):
        spread = jnp.broadcast_to(jnp.concatenate(row, axis=1), (count, 2 * count))
        spread = pltpu.roll(spread, 0, 1, stride=1, stride_axis=0)
        wt_ref[half * count : (half + 1) * count, :] = spread[:, :count].astype(jnp.bfloat16)


def parameter_table(harmonic, col_scale):
    rows = [harmonic >> 6, harmonic & 63]
    rows = [x.astype(jnp.float32) for x in rows] + [col_scale * (math.sqrt(2.0) * LEAD)]
    return jnp.concatenate(rows + [jnp.zeros((125, harmonic.shape[1]), jnp.float32)]).T


def fill_design(h_ref, pt_ref, d_ref, start, stop, lane, tile):
    here = slice(start, stop)
    p0 = pt_ref[0:1, pl.ds(tile, 256)]
    p1 = pt_ref[1:2, pl.ds(tile, 256)]
    turns = h_ref[here, 0:1] * p0 + h_ref[here, 1:2] * p1 - 0.125
    s = 0.25 - jnp.abs(turns - jnp.round(turns))
    z = s * s
    poly = ((z + POLY[2]) * z + POLY[1]) * z + POLY[0]
    d_ref[here, lane : lane + 256] = (poly * (s * h_ref[here, 2:3])).astype(jnp.bfloat16)


def fill_filtered(d_ref, wt_ref, f_ref, start, stop, block):
    count = wt_ref.shape[1]
    f_ref[start:stop, block * count : (block + 1) * count] = jnp.dot(
        d_ref[start:stop, block * count : (block + 2) * count],
        wt_ref[...],
        preferred_element_type=jnp.float32,
    ).astype(jnp.bfloat16)


def fill_lead(h_ref, pt_ref, wt_ref, d_ref, lead_ref, block_ref):
    tiles, lead, tile = lead_ref.shape
    epochs = pt_ref.shape[1]
    count = wt_ref.shape[1]
    blocks = tile // count
    d_ref[:, :count] = jnp.zeros((lead, count), jnp.bfloat16)
    block_ref[...] = jnp.zeros_like(block_ref)

    def design(start, block):
        for row in range(0, lead, 16):
            fill_design(
                h_ref, pt_ref, d_ref, row, row + 16, (block + 1) * count, start + block * count
            )

    for b in range(blocks):
        design(0, b)

    @pl.loop(0, tiles, unroll=2 - tiles % 2)
    def _(step):
        following = pl.multiple_of(lax.rem((step + 1) * tile, epochs), tile)
        out_ref = lead_ref.at[step]
        for b in range(blocks):
            fill_filtered(d_ref, wt_ref, out_ref, 0, lead, b)
            if b == min(1, blocks - 1):
                d_ref[:, :count] = d_ref[:, tile:]
            if b > 0:
                if b == blocks - 1:
                    block_ref[...] += lax.dot_general(
                        out_ref[...],
                        out_ref[...],
                        (((1,), (1,)), ((), ())),
                        preferred_element_type=jnp.float32,
                    )
                design(following, b - 1)
        design(following, blocks - 1)


def main_kernel(shape, *refs):
    rows, lead, cols, n_epoch, n_row = shape
    parts_refs, refs = refs[:n_epoch], refs[n_epoch:]
    harmonic_ref, scale_ref, taps_ref, ridge_ref, panel_out, schur_out = refs[:6]
    sums_ref, pt_ref, wt_ref, dl_ref, lead_ref, block_ref = refs[6:12]
    h_ref, r_ref, d_ref, fa_ref, fb_ref, acc_ref, m_ref, first_ref = refs[12:20]
    panel_ref, schur_ref, sem = refs[20:]
    width, tile = fa_ref.shape
    count = wt_ref.shape[1]
    step = pl.program_id(0)
    epochs = pt_ref.shape[1]
    mine = lax.axis_index("epoch") * n_row + lax.axis_index("prow")
    first_row = pl.multiple_of(mine * rows, rows)
    first_col = pl.multiple_of(lax.axis_index("pcol") * cols, cols)
    segments = [(0, rows), (rows + lead, width)]
    chunks = [(at, min(at + 256, stop)) for start, stop in segments for at in range(start, stop, 256)]
    n_lead_chunks = -(-rows // 256)

    def design(start, row):
        def run():
            d_ref[row : row + 16, :count] = d_ref[row : row + 16, tile:]
            for lane in range(0, tile, 256):
                fill_design(h_ref, pt_ref, d_ref, row, row + 16, count + lane, start + lane)
        return run

    def filtered(f_ref, begin, end, block):
        return lambda: fill_filtered(d_ref, wt_ref, f_ref, begin, end, block)

    def product(f_ref, begin, end, depth):
        def run():
            acc_ref[:depth, begin:end] += lax.dot_general(
                f_ref[:depth, :],
                f_ref[rows + begin : rows + end, :],
                (((1,), (1,)), ((), ())),
                preferred_element_type=jnp.float32,
            )
        return run

    def products(f_ref):
        pieces = [(0, lead, rows)]
        pieces += [(c, min(c + 256, lead + cols), rows + lead) for c in range(lead, lead + cols, 256)]
        return [(product(f_ref, *p), (p[1] - p[0]) * p[2] * tile) for p in pieces]

    @pl.when(step == 0)
    def _():
        fill_phases(lax.axis_index("epoch"), parts_refs, sums_ref, pt_ref)
        fill_toeplitz(taps_ref, wt_ref)
        if rows % 128 or cols % 128:
            r_ref[...] = parameter_table(harmonic_ref[...], scale_ref[...])
            h_ref[:rows, :] = r_ref[pl.ds(first_row, rows), :]
            h_ref[rows + lead :, :] = r_ref[pl.ds(first_col, cols), :]
        else:
            for at, first, size in ((0, first_row, rows), (rows + lead, first_col, cols)):
                span = pl.ds(first, size)
                h_ref[at : at + size, :] = parameter_table(harmonic_ref[:, span], scale_ref[:, span])
            r_ref[:lead, :] = parameter_table(harmonic_ref[:, :lead], scale_ref[:, :lead])
        fill_lead(r_ref, pt_ref, wt_ref, dl_ref, lead_ref, block_ref)
        acc_ref[...] = jnp.zeros_like(acc_ref)
        d_ref[...] = jnp.zeros_like(d_ref)
        first = []
        local = parts_refs[0].shape[1]
        deep = -(-rows // local)
        for q in range(-(-lead // rows)):
            total = jnp.zeros((1, rows), jnp.float32)
            for e, ref in enumerate(parts_refs):
                for k in range(n_row):
                    group = lax.rem(lax.axis_index("epoch") - e + n_epoch, n_epoch)
                    row_group = lax.rem(lax.axis_index("prow") - k + n_row, n_row)
                    held = [ref[2 + k * deep + d : 3 + k * deep + d, :] for d in range(deep)]
                    held = jnp.concatenate(held, axis=1)[:, :rows]
                    found = (group == q // n_row) & (row_group == q % n_row)
                    total = total + jnp.where(found, held, 0.0)
            first.append(total)
        first = jnp.concatenate(first, axis=1)[:, :lead]
        first_ref[...] = jnp.concatenate([first, jnp.zeros((127, lead), jnp.float32)]).T
        i = lax.broadcasted_iota(jnp.int32, (lead, lead), 0)
        j = lax.broadcasted_iota(jnp.int32, (lead, lead), 1)
        m_ref[...] = block_ref[...] * (1.0 / epochs) + jnp.where(i == j, first_ref[:, :1], 0.0)
        for begin, end in segments:
            for row in range(begin, end, 16):
                design(0, row)()

    def phase(f_ref, half, extra):
        following = pl.multiple_of(lax.rem((2 * step + half + 1) * tile, epochs), tile)
        f_ref[rows : rows + lead, :] = lead_ref[step, :, half * tile : (half + 1) * tile]
        work, ready = [], []

        def filters(begin, end):
            for b in range(tile // count):
                work.append((filtered(f_ref, begin, end, b), (end - begin) * 2 * count * count, None))
            work[-1] = (*work[-1][:2], range(begin, end, 16))

        pieces = products(f_ref)
        for begin, end in chunks[:n_lead_chunks]:
            filters(begin, end)
        for n, (begin, end) in enumerate(chunks[n_lead_chunks:]):
            filters(begin, end)
            work.append((*pieces[n], None))
        for piece in pieces[len(chunks) - n_lead_chunks :]:
            work.append((*piece, None))
        total, spent, given = sum(w[1] for w in work), 0, 0
        every = sum(end - begin for begin, end in chunks) // 16
        for run, cost, rows_done in work:
            run()
            spent += cost
            ready += list(rows_done or ())
            while given < every * spent // total and ready:
                design(following, ready.pop(0))()
                next(extra, None)
                given += 1
        for row in ready:
            design(following, row)()
            next(extra, None)

    always = epochs // (2 * tile) <= lead // FACTOR_BLOCK
    factor = factor_step(m_ref, step, FACTOR_BLOCK, FACTOR_GROUP, always)
    phase(fa_ref, 0, factor)
    phase(fb_ref, 1, factor)
    for _ in factor:
        pass

    @pl.when(step == pl.num_programs(0) - 1)
    def _():
        mid = -(-rows // 128) * 128
        own = ridge_ref[...]
        if mid > rows:
            own = jnp.concatenate([own, jnp.zeros((1, mid - rows), jnp.float32)], axis=1)
        own = jnp.concatenate([own, jnp.zeros((127, mid), jnp.float32)]).T[:rows, :1]
        first = first_ref[:, :1]
        scale = 1.0 / epochs
        @pl.loop(epochs // (2 * tile), max(lead // FACTOR_BLOCK, epochs // (2 * tile)))
        def _(k):
            for _ in factor_step(m_ref, k, FACTOR_BLOCK, FACTOR_GROUP, True):
                pass

        def total(begin, end, first, width_of, first_id, diagonal):
            i = lax.broadcasted_iota(jnp.int32, (end - begin, width_of), 0)
            j = lax.broadcasted_iota(jnp.int32, (end - begin, width_of), 1) + first_id
            i = i + first_row if begin == 0 else i
            block = acc_ref[begin:end, first : first + width_of]
            return block * scale + jnp.where(i == j, diagonal, 0.0)

        i = lax.broadcasted_iota(jnp.int32, (lead, lead), 0)
        j = lax.broadcasted_iota(jnp.int32, (lead, lead), 1)
        inverse = split3(jnp.where(i >= j, m_ref[...], 0.0))
        panel = product_f32(split3(total(0, rows, 0, lead, 0, own)), inverse, 1)
        panel_ref[...] = panel
        copies = [pltpu.make_async_copy(panel_ref, panel_out, sem.at[0])]
        copies[0].start()
        panel = split3(panel)
        for n, c in enumerate(range(0, cols, 256)):
            size = min(256, cols - c)
            span = slice(c, c + size)
            right = total(rows, rows + lead, lead + c, size, first_col + c, first)
            solved = split3(product_f32(inverse, split3(right), 0))
            left = total(0, rows, lead + c, size, first_col + c, own)
            schur_ref[:, span] = left - product_f32(panel, solved, 0)
            copies.append(
                pltpu.make_async_copy(schur_ref.at[:, span], schur_out.at[:, span], sem.at[n + 1])
            )
            copies[-1].start()
        for copy in copies:
            copy.wait()


def on_device(steps, harmonic, col_scale, taps, ridge):
    params = harmonic.shape[0]
    n_epoch = lax.axis_size("epoch")
    n_row = lax.axis_size("prow")
    n_col = lax.axis_size("pcol")
    rows = params // (n_epoch * n_row)
    cols = params // n_col
    width = rows + B + cols
    epochs = steps.shape[1] * n_epoch
    count = taps.shape[0]
    tile = 512
    here = steps.shape[1]
    ridge_rows = -(-rows // here)
    packed = jnp.pad(steps, ((0, n_row * ridge_rows), (0, 0))).astype(jnp.float32)
    for k, x in enumerate(rotated(ridge, "prow")):
        x = jnp.pad(x, (0, ridge_rows * here - rows)).reshape(ridge_rows, here)
        packed = packed + jnp.pad(x, ((2 + k * ridge_rows, (n_row - 1 - k) * ridge_rows), (0, 0)))
    parts = rotated(packed, "epoch")
    row_of = lambda x: x.reshape(1, -1)
    in_vmem = pl.BlockSpec(memory_space=pltpu.VMEM)
    f32 = lambda *shape: jax.ShapeDtypeStruct(shape, jnp.float32)
    operands = (*parts, row_of(harmonic), row_of(col_scale), row_of(taps), row_of(ridge))
    vmem = lambda dtype, *shape: pltpu.VMEM(shape, dtype)
    return pl.pallas_call(
        functools.partial(main_kernel, (rows, B, cols, n_epoch, n_row)),
        grid=(epochs // (2 * tile),),
        out_shape=(f32(rows, B), f32(rows, cols)),
        in_specs=[in_vmem] * len(operands),
        out_specs=(pl.BlockSpec(memory_space=pl.ANY),) * 2,
        scratch_shapes=[
            vmem(jnp.float32, 2 * epochs // 128, 128),
            vmem(jnp.float32, 8, epochs),
            vmem(jnp.bfloat16, 2 * count, count),
            vmem(jnp.bfloat16, B, count + 2 * tile),
            vmem(jnp.bfloat16, epochs // (2 * tile), B, 2 * tile),
            vmem(jnp.float32, B, B),
            vmem(jnp.float32, width, 128),
            vmem(jnp.float32, params, 128),
            vmem(jnp.bfloat16, width, count + tile),
            vmem(jnp.bfloat16, width, tile),
            vmem(jnp.bfloat16, width, tile),
            vmem(jnp.float32, rows + B, B + cols),
            vmem(jnp.float32, B, B),
            vmem(jnp.float32, B, 128),
            vmem(jnp.float32, rows, B),
            vmem(jnp.float32, rows, cols),
            pltpu.SemaphoreType.DMA((1 + -(-cols // 256),)),
        ],
        compiler_params=pltpu.CompilerParams(vmem_limit_bytes=VMEM_LIMIT),
    )(*operands)


def solution(mesh):
    in_specs = (P(None, "epoch"), P(), P(), P(), P(("epoch", "prow")))
    out_specs = (P(("epoch", "prow"), None), P(("epoch", "prow"), "pcol"))
    return jax.shard_map(
        on_device, mesh=mesh, in_specs=in_specs, out_specs=out_specs, check_vma=False
    )
```
